256 devices in a mesh: dp: 16 (over z_lo, y, core), shard: 16 (over z_hi, x).
Axes of the slice: x: 4, y: 4, z: 8 (z_hi: 4, z_lo: 2; z = z_hi * 2 + z_lo), core: 2. Of those that a mesh axis runs over, the one named last changes fastest.
Arguments:
- grads: bfloat16 [16, 18, 7168, 128], P('dp', None, 'shard'), may hold values from -230 to 230
- params: float32 [18, 7168, 128], P(None, 'shard'), may hold values from -6 to 6
- table: int32 [18], replicated, may hold values from 0 to 17, each once
Outputs:
- new_params: float32 [18, 7168, 128], P(None, 'shard')
- update: bfloat16 [18, 7168, 128], P(None, 'shard')
The draws below stay inside these ranges and needn't reach their ends.
Inputs may be any that keep to these rules, and one draw needn't show every extreme that they name: A permutation: gradient block j belongs to head table[j].
All inputs are finite; a program needn't handle non-finite values.
Results may differ from the reference program's by a relative error of at most 0.006.
Values may be sent and summed in bfloat16 or wider, within the bound.
A program may use at most 64 MiB of HBM per device.

```python
import math
import jax
import jax.numpy as jnp
from jax import lax

D = 7168
V = 128
NMAT = 18
ITERS = 5
N_DP = 16


def draw_grads(key, part):
    key = jax.random.fold_in(key, 5)
    keys = jax.random.split(key, 3)
    shape = (N_DP, NMAT, D, V)
    base = jnp.clip(jax.random.normal(keys[0], shape, jnp.float32), -5.0, 5.0)
    row_scale = jnp.exp(jax.random.uniform(keys[1], (1, NMAT, D, 1), jnp.float32, 0.0, math.log(10.0)))
    row_rise = jnp.exp(math.log(3.0) * jnp.arange(D, dtype=jnp.float32) / D).reshape(1, 1, D, 1)
    col_scale = jnp.exp(jax.random.uniform(keys[2], (1, 1 * NMAT, 1, V), jnp.float32, 0.0, math.log(10.0)))
    replica_rise = jnp.exp(math.log(3.0) * jnp.arange(N_DP, dtype=jnp.float32) / max(N_DP - 1, 1)).reshape(N_DP, 1, 1, 1)
    values = 0.05 * base * row_scale * row_rise * col_scale * replica_rise
    return values.astype(jnp.bfloat16)


def level_of(own_key, dims, cuts, smallest, high):
    def one(position, shards_of):
        heights = jax.random.uniform(jax.random.fold_in(jax.random.fold_in(own_key, 6), position), (shards_of,), jnp.float32, smallest / len(cuts), high / len(cuts))
        return jnp.repeat(jnp.exp(heights), dims[position] // shards_of).reshape((-1,) + (1,) * (len(dims) - position - 1))

    factor_of = one(*cuts[0])
    for cut in cuts[1:]:
        factor_of = factor_of * one(*cut)
    return factor_of


def gaussian(key, shape, scale, bound, cuts=(), kind=jnp.bfloat16):
    result = scale * jax.random.normal(key, shape, jnp.float32)
    if cuts:
        result = result * level_of(key, shape, cuts, -0.22, 0.18)
    return jnp.clip(result, -bound, bound).astype(kind)


def setup_inputs(seed: int = 0) -> dict:
    streams_of = jax.random.split(jax.random.key(seed), 4)
    return {
        "grads": draw_grads(jax.random.fold_in(streams_of[3], 71), 0),
        "params": gaussian(streams_of[1], (NMAT, D, V), 1.0, 6.0, ((1, 16),), jnp.float32),
        "table": jax.random.permutation(streams_of[2], NMAT).astype(jnp.int32),
    }


quintic_one = 3.4445
quintic_two = -4.775
quintic_three = 2.0315
epsilon = 1e-07
learning_rate = 0.02
decay_rate = 0.1

def orthogonal_one(block):
    wide = block.astype(jnp.float32)
    norm_value = jnp.sqrt(jnp.sum(wide * wide))
    current = wide / (norm_value + epsilon)
    for index in range(ITERS):
        gram = jnp.dot(current.T, current, precision=lax.Precision.HIGHEST, preferred_element_type=jnp.float32)
        poly = quintic_two * gram + quintic_three * jnp.dot(gram, gram, precision=lax.Precision.HIGHEST, preferred_element_type=jnp.float32)
        current = quintic_one * current + jnp.dot(current, poly, precision=lax.Precision.HIGHEST, preferred_element_type=jnp.float32)
    return current.astype(jnp.bfloat16)

def reference(grads, params, table):
    total = jnp.zeros(grads.shape[1:], jnp.float32)
    for index in range(N_DP):
        total = total + grads[index].astype(jnp.float32)
    blocks = total.astype(jnp.bfloat16)
    ortho = lax.map(orthogonal_one, blocks)
    heads = jnp.zeros_like(ortho).at[table].set(ortho)
    scaled = 0.2 * math.sqrt(max(D, V)) * heads.astype(jnp.float32)
    new_params = params - learning_rate * (scaled + decay_rate * params)
    return (new_params, scaled.astype(jnp.bfloat16))
```

```python
import functools
import math

import jax
import jax.numpy as jnp
from jax import lax
from jax.experimental import pallas as pl
from jax.experimental.pallas import tpu as pltpu
from jax.sharding import PartitionSpec as P

D = 7168
V = 128
ITERS = 5
N_DP = 16
N_SHARD = 16
CHIPS = 8
CHUNKS = 4
TAIL_OWNERS = 14

quintic_one = 3.4445
quintic_two = -4.775
quintic_three = 2.0315
epsilon = 1e-07
learning_rate = 0.02
decay_rate = 0.1

MESH = pl.DeviceIdType.MESH
HIGHEST = lax.Precision.HIGHEST


def exact_dot(left, right):
    return jnp.dot(left, right, precision=HIGHEST, preferred_element_type=jnp.float32)


def identity_matrix():
    rows = lax.broadcasted_iota(jnp.int32, (V, V), 0)
    cols = lax.broadcasted_iota(jnp.int32, (V, V), 1)
    return (rows == cols).astype(jnp.float32)


def gram_of(rows):
    return lax.dot_general(
        rows, rows, (((0,), (0,)), ((), ())), preferred_element_type=jnp.float32
    )


def polynomial_of(total_gram, between):
    eye = identity_matrix()
    square = jnp.sum(jnp.sum(total_gram * eye, axis=1, keepdims=True), axis=0, keepdims=True)
    inverse = 1.0 / (jnp.sqrt(square) + epsilon)
    gram = (total_gram * inverse) * inverse
    product = None
    for index in range(ITERS):
        step = quintic_one * eye + quintic_two * gram + quintic_three * exact_dot(gram, gram)
        if index == ITERS - 1:
            product = exact_dot(product, step)
        elif index == 0:
            product = step
            gram = exact_dot(exact_dot(gram, step), step)
        else:
            both = exact_dot(jnp.concatenate([gram, product], axis=0), step)
            product = both[V:]
            gram = exact_dot(both[:V], step)
        between(index)
    return product * inverse


def communicate(
    grads, x_out, p_out,
    pieces, tail_pieces, own, tail, grams, gram_parts, gram_full, result,
    piece_sems, piece_send, tail_sem, tail_send, tailx_sem, tailx_send,
    gram_sems, gram_send, x_sems, x_send, p_sems, p_send, local_sem, tailp_sem, tailp_send,
    *, count, rows,
):
    part = rows // CHUNKS
    blocks = N_DP
    tail_rows = (count - blocks) * rows
    tail_piece = tail_rows // TAIL_OWNERS
    me = lax.axis_index("dp")
    shard = lax.axis_index("shard")
    core = lax.rem(me, 2)
    chip = me // 2
    half = me // 8
    sibling = me + 1 - 2 * core

    def chip_at(offset):
        z = lax.rem(chip // 4 + offset // 4, 2)
        y = lax.rem(lax.rem(chip, 4) + offset % 4, 4)
        return 4 * z + y

    def chip_before(offset):
        z = lax.rem(chip // 4 + offset // 4, 2)
        y = lax.rem(lax.rem(chip, 4) + 4 - offset % 4, 4)
        return 4 * z + y

    barrier = pltpu.get_barrier_semaphore()

    def greet(step, carry):
        pl.semaphore_signal(
            barrier, inc=1, device_id={"dp": lax.rem(me + step, N_DP)}, device_id_type=MESH
        )
        pl.semaphore_signal(
            barrier, inc=1, device_id={"shard": lax.rem(shard + step, N_SHARD)}, device_id_type=MESH
        )
        return carry

    lax.fori_loop(1, N_DP, greet, 0)
    own_copies = []
    for chunk in range(CHUNKS):
        copy = pltpu.make_async_copy(
            grads.at[pl.ds(me * rows + chunk * part, part)],
            pieces.at[chunk, me],
            piece_sems.at[chunk],
        )
        copy.start()

    @pl.when(me < TAIL_OWNERS)
    def _():
        pltpu.make_async_copy(
            grads.at[pl.ds(blocks * rows + me * tail_piece, tail_piece)],
            tail_pieces.at[me],
            tail_sem,
        ).start()

    pl.semaphore_wait(barrier, N_DP - 1 + N_SHARD - 1)

    def send_tail(step, carry):
        peer = lax.rem(me + step, N_DP)

        @pl.when(peer < TAIL_OWNERS)
        def _():
            pltpu.make_async_remote_copy(
                src_ref=grads.at[pl.ds(blocks * rows + peer * tail_piece, tail_piece)],
                dst_ref=tail_pieces.at[me],
                send_sem=tail_send,
                recv_sem=tail_sem,
                device_id={"dp": peer},
                device_id_type=MESH,
            ).start()

        return carry

    lax.fori_loop(1, N_DP, send_tail, 0)

    def send_piece(peer, chunk):
        pltpu.make_async_remote_copy(
            src_ref=grads.at[pl.ds(peer * rows + chunk * part, part)],
            dst_ref=pieces.at[chunk, me],
            send_sem=piece_send,
            recv_sem=piece_sems.at[chunk],
            device_id={"dp": peer},
            device_id_type=MESH,
        ).start()

    for chunk in range(CHUNKS):
        def send_pieces(offset, carry, chunk=chunk):
            other = chip_at(offset)
            send_piece(2 * other + core, chunk)
            send_piece(2 * other + 1 - core, chunk)
            return carry

        lax.fori_loop(1, CHIPS, send_pieces, 0)
        send_piece(sibling, chunk)

    @pl.when(me < TAIL_OWNERS)
    def _():
        pltpu.make_async_copy(tail_pieces, tail_pieces, tail_sem).wait()
        total = tail_pieces[0].astype(jnp.float32)
        for source in range(1, N_DP):
            total = total + tail_pieces[source].astype(jnp.float32)
        tail[pl.ds(me * tail_piece, tail_piece)] = total.astype(jnp.bfloat16)

        def spread(step, carry):
            here = tail.at[pl.ds(me * tail_piece, tail_piece)]
            pltpu.make_async_remote_copy(
                src_ref=here,
                dst_ref=here,
                send_sem=tailx_send,
                recv_sem=tailx_sem,
                device_id={"dp": lax.rem(me + step, N_DP)},
                device_id_type=MESH,
            ).start()
            return carry

        lax.fori_loop(1, N_DP, spread, 0)
        most = tail.at[pl.ds(0, (TAIL_OWNERS - 1) * tail_piece)]
        pltpu.make_async_copy(most, most, tailx_sem).wait()

    @pl.when(me >= TAIL_OWNERS)
    def _():
        pltpu.make_async_copy(tail, tail, tailx_sem).wait()

    tail_copy = pltpu.make_async_copy(tail, x_out.at[pl.ds(blocks * rows, tail_rows)], local_sem.at[0])
    tail_copy.start()

    def gram_start(which, gram):
        grams[which] = gram
        gram_parts[which, shard] = grams[which, pl.ds(shard * 8, 8)]

        def send(step, carry):
            peer = lax.rem(shard + step, N_SHARD)
            pltpu.make_async_remote_copy(
                src_ref=grams.at[which, pl.ds(peer * 8, 8)],
                dst_ref=gram_parts.at[which, shard],
                send_sem=gram_send.at[which, 0],
                recv_sem=gram_sems.at[which, 0],
                device_id={"shard": peer},
                device_id_type=MESH,
            ).start()
            return carry

        lax.fori_loop(1, N_SHARD, send, 0)

    def gram_finish(which):
        most = gram_parts.at[which, pl.ds(0, N_SHARD - 1)]
        pltpu.make_async_copy(most, most, gram_sems.at[which, 0]).wait()
        gram_full[which, pl.ds(shard * 8, 8)] = jnp.sum(gram_parts[which], axis=0)

        def send(step, carry):
            here = gram_full.at[which, pl.ds(shard * 8, 8)]
            pltpu.make_async_remote_copy(
                src_ref=here,
                dst_ref=here,
                send_sem=gram_send.at[which, 1],
                recv_sem=gram_sems.at[which, 1],
                device_id={"shard": lax.rem(shard + step, N_SHARD)},
                device_id_type=MESH,
            ).start()
            return carry

        lax.fori_loop(1, N_SHARD, send, 0)
        most = gram_full.at[which, pl.ds(0, (N_SHARD - 1) * 8)]
        pltpu.make_async_copy(most, most, gram_sems.at[which, 1]).wait()

    gram_start(0, gram_of(tail[pl.ds(half * rows, rows)]))
    gram_finish(0)
    result[0] = polynomial_of(gram_full[0], lambda index: None)
    tail_slot = blocks + half
    pltpu.make_async_copy(result.at[0], p_out.at[tail_slot], local_sem.at[1]).start()
    other_half = lax.rem(me + 8, N_DP)
    tail_p = pltpu.make_async_remote_copy(
        src_ref=result.at[0],
        dst_ref=p_out.at[tail_slot],
        send_sem=tailp_send,
        recv_sem=tailp_sem,
        device_id={"dp": other_half},
        device_id_type=MESH,
    )
    tail_p.start()

    for chunk in range(CHUNKS):
        pltpu.make_async_copy(pieces.at[chunk], pieces.at[chunk], piece_sems.at[chunk]).wait()
        total = pieces[chunk, 0].astype(jnp.float32)
        for source in range(1, N_DP):
            total = total + pieces[chunk, source].astype(jnp.float32)
        summed = total.astype(jnp.bfloat16)
        own[pl.ds(chunk * part, part)] = summed
        gram = gram_of(summed)
        grams[1] = gram if chunk == 0 else grams[1] + gram
    gram_start(1, grams[1])

    here = x_out.at[pl.ds(me * rows, rows)]
    pltpu.make_async_copy(own, here, local_sem.at[2]).start()

    def x_copy(peer, slot):
        return pltpu.make_async_remote_copy(
            src_ref=own,
            dst_ref=here,
            send_sem=x_send.at[0],
            recv_sem=x_sems.at[slot],
            device_id={"dp": peer},
            device_id_type=MESH,
        )

    def send_x(offset, carry):
        x_copy(2 * chip_at(offset) + core, offset).start()
        return carry

    lax.fori_loop(1, CHIPS, send_x, 0)
    x_copy(sibling, 0).start()

    gram_finish(1)

    def pass_x(offset):
        source = 2 * chip_before(offset) + core
        place = x_out.at[pl.ds(source * rows, rows)]
        pltpu.make_async_copy(place, place, x_sems.at[offset]).wait()
        pltpu.make_async_remote_copy(
            src_ref=place,
            dst_ref=place,
            send_sem=x_send.at[1],
            recv_sem=x_sems.at[CHIPS + offset],
            device_id={"dp": sibling},
            device_id_type=MESH,
        ).start()

    def between(index):
        for offset in ((1, 3), (4,), (2, 5), (7,), (6,))[index]:
            pass_x(offset)

    result[1] = polynomial_of(gram_full[1], between)

    pltpu.make_async_copy(result.at[1], p_out.at[me], local_sem.at[3]).start()

    def p_copy(peer, slot):
        return pltpu.make_async_remote_copy(
            src_ref=result.at[1],
            dst_ref=p_out.at[me],
            send_sem=p_send.at[0],
            recv_sem=p_sems.at[slot],
            device_id={"dp": peer},
            device_id_type=MESH,
        )

    def send_p(offset, carry):
        p_copy(2 * chip_at(offset) + core, offset).start()
        return carry

    lax.fori_loop(1, CHIPS, send_p, 0)
    p_copy(sibling, 0).start()
    for offset in (1, 3, 4, 2, 5, 7, 6):
        source = 2 * chip_before(offset) + core
        place = p_out.at[source]
        pltpu.make_async_copy(place, place, p_sems.at[offset]).wait()
        pltpu.make_async_remote_copy(
            src_ref=place,
            dst_ref=place,
            send_sem=p_send.at[1],
            recv_sem=p_sems.at[CHIPS + offset],
            device_id={"dp": sibling},
            device_id_type=MESH,
        ).start()

    sibling_block = x_out.at[pl.ds(sibling * rows, rows)]
    pltpu.make_async_copy(sibling_block, sibling_block, x_sems.at[0]).wait()
    pltpu.make_async_copy(p_out.at[sibling], p_out.at[sibling], p_sems.at[0]).wait()
    for offset in range(1, CHIPS):
        source = 2 * chip_before(offset) + 1 - core
        place = x_out.at[pl.ds(source * rows, rows)]
        pltpu.make_async_copy(place, place, x_sems.at[CHIPS + offset]).wait()
        pltpu.make_async_copy(p_out.at[source], p_out.at[source], p_sems.at[CHIPS + offset]).wait()
    tail_p.wait()
    tail_copy.wait()
    pltpu.make_async_copy(result.at[0], p_out.at[tail_slot], local_sem.at[1]).wait()
    pltpu.make_async_copy(own, here, local_sem.at[2]).wait()
    pltpu.make_async_copy(result.at[1], p_out.at[me], local_sem.at[3]).wait()

    def sent(ref, sem):
        pltpu.make_async_copy(ref, ref, sem).wait()

    sent(grads.at[pl.ds(0, (N_DP - 1) * rows)], piece_send)

    @pl.when(me < TAIL_OWNERS)
    def _():
        sent(tail_pieces.at[pl.ds(0, TAIL_OWNERS - 1)], tail_send)
        sent(tail_pieces.at[pl.ds(0, N_DP - 1)], tailx_send)

    @pl.when(me >= TAIL_OWNERS)
    def _():
        sent(tail_pieces.at[pl.ds(0, TAIL_OWNERS)], tail_send)

    for which in range(2):
        sent(gram_parts.at[which, pl.ds(0, N_SHARD - 1)], gram_send.at[which, 0])
        sent(gram_parts.at[which, pl.ds(0, N_SHARD - 1)], gram_send.at[which, 1])
    sent(x_out.at[pl.ds(0, CHIPS * rows)], x_send.at[0])
    sent(x_out.at[pl.ds(0, (CHIPS - 1) * rows)], x_send.at[1])
    sent(p_out.at[pl.ds(0, CHIPS)], p_send.at[0])
    sent(p_out.at[pl.ds(0, CHIPS - 1)], p_send.at[1])


def exchange(flat, count, rows):
    part = rows // CHUNKS
    tail_rows = (count - N_DP) * rows
    dma = pltpu.SemaphoreType.DMA
    return pl.pallas_call(
        functools.partial(communicate, count=count, rows=rows),
        out_shape=(
            jax.ShapeDtypeStruct((count * rows, V), jnp.bfloat16),
            jax.ShapeDtypeStruct((count, V, V), jnp.float32),
        ),
        in_specs=[pl.BlockSpec(memory_space=pl.ANY)],
        out_specs=(pl.BlockSpec(memory_space=pl.ANY), pl.BlockSpec(memory_space=pl.ANY)),
        scratch_shapes=[
            pltpu.VMEM((CHUNKS, N_DP, part, V), jnp.bfloat16),
            pltpu.VMEM((N_DP, tail_rows // TAIL_OWNERS, V), jnp.bfloat16),
            pltpu.VMEM((rows, V), jnp.bfloat16),
            pltpu.VMEM((tail_rows, V), jnp.bfloat16),
            pltpu.VMEM((2, V, V), jnp.float32),
            pltpu.VMEM((2, N_SHARD, 8, V), jnp.float32),
            pltpu.VMEM((2, V, V), jnp.float32),
            pltpu.VMEM((2, V, V), jnp.float32),
            dma((CHUNKS,)), dma, dma, dma, dma, dma,
            dma((2, 2)), dma((2, 2)),
            dma((2 * CHIPS,)), dma((2,)),
            dma((2 * CHIPS,)), dma((2,)),
            dma((4,)), dma, dma,
        ],
        compiler_params=pltpu.CompilerParams(
            collective_id=0, has_side_effects=True, vmem_limit_bytes=32 * 2**20
        ),
    )(flat)


def finish(table, x, p, params, new_params, update):
    matrix = p[0]
    high = matrix.astype(jnp.bfloat16)
    low = (matrix - high.astype(jnp.float32)).astype(jnp.bfloat16)
    block = x[0]
    whole = jnp.dot(
        jnp.concatenate([block, block], axis=1),
        jnp.concatenate([high, low], axis=0),
        preferred_element_type=jnp.float32,
    )
    scaled = 0.2 * math.sqrt(max(D, V)) * whole.astype(jnp.bfloat16).astype(jnp.float32)
    old = params[0]
    new_params[0] = old - learning_rate * (scaled + decay_rate * old)
    update[0] = scaled.astype(jnp.bfloat16)


def apply(table, x, p, params):
    count, rows, width = params.shape
    place = lambda j, table: (table[j], 0, 0)
    mine = lambda j, table: (j, 0, 0)
    return pl.pallas_call(
        finish,
        grid_spec=pltpu.PrefetchScalarGridSpec(
            num_scalar_prefetch=1,
            grid=(count,),
            in_specs=[
                pl.BlockSpec((1, rows, width), mine),
                pl.BlockSpec((1, width, width), mine),
                pl.BlockSpec((1, rows, width), place),
            ],
            out_specs=[
                pl.BlockSpec((1, rows, width), place),
                pl.BlockSpec((1, rows, width), place),
            ],
        ),
        out_shape=(
            jax.ShapeDtypeStruct((count, rows, width), jnp.float32),
            jax.ShapeDtypeStruct((count, rows, width), jnp.bfloat16),
        ),
        compiler_params=pltpu.CompilerParams(vmem_limit_bytes=32 * 2**20),
    )(table, x.reshape(count, rows, width), p, params)


def per_device(grads, params, table):
    count, rows, width = params.shape
    x, p = exchange(grads.reshape(count * rows, width), count, rows)
    return apply(table, x, p, params)


def solution(mesh):
    return jax.shard_map(
        per_device,
        mesh=mesh,
        in_specs=(P("dp", None, "shard", None), P(None, "shard", None), P()),
        out_specs=(P(None, "shard", None), P(None, "shard", None)),
        check_vma=False,
    )
```

```python
import functools
import math

import jax
import jax.numpy as jnp
from jax import lax
from jax.experimental import pallas as pl
from jax.experimental.pallas import tpu as pltpu
from jax.sharding import PartitionSpec as P

D = 7168
V = 128
HALF = V // 2
PACKED = HALF + 8
ITERS = 5
N_DP = 16
CHIPS = 8
TAIL_OWNERS = 7
CODE_MAX = 32767.0

quintic_one = 3.4445
quintic_two = -4.775
quintic_three = 2.0315
epsilon = 1e-07
learning_rate = 0.02
decay_rate = 0.1

MESH = pl.DeviceIdType.MESH
HIGHEST = lax.Precision.HIGHEST


def exact_dot(left, right):
    return jnp.dot(left, right, precision=HIGHEST, preferred_element_type=jnp.float32)


def places(rows):
    return (
        lax.broadcasted_iota(jnp.int32, (rows, V), 0),
        lax.broadcasted_iota(jnp.int32, (rows, V), 1),
    )


def gram_of(rows):
    return lax.dot_general(
        rows, rows, (((0,), (0,)), ((), ())), preferred_element_type=jnp.float32
    )


def pack(matrix):
    row, col = places(HALF)
    corner = pltpu.roll(matrix[HALF:], HALF, 1)
    body = jnp.where((col < HALF) & (row > col), corner, matrix[:HALF])
    diagonal = jnp.sum(jnp.where(row == col, corner, 0.0), axis=0, keepdims=True)
    return jnp.concatenate([body, jnp.broadcast_to(diagonal, (8, V))], axis=0)


def unpack(packed):
    row, col = places(HALF)
    body, diagonal = packed[:HALF], packed[HALF:HALF + 1]
    turned = jnp.concatenate([body, jnp.zeros_like(body)], axis=0).T
    top = jnp.where((col < HALF) & (row > col), turned[:HALF], body)
    corner = jnp.where(row > col, body, jnp.where(row < col, turned[:HALF], diagonal))
    bottom = jnp.where(col < HALF, turned[HALF:], pltpu.roll(corner, HALF, 1))
    return jnp.concatenate([top, bottom], axis=0)


def polynomial_of(total_gram, between):
    row, col = places(V)
    eye = (row == col).astype(jnp.float32)
    square = jnp.sum(jnp.sum(total_gram * eye, axis=1, keepdims=True), axis=0, keepdims=True)
    inverse = 1.0 / (jnp.sqrt(square) + epsilon)
    gram = (total_gram * inverse) * inverse
    product = None
    for index in range(ITERS):
        step = quintic_one * eye + quintic_two * gram + quintic_three * exact_dot(gram, gram)
        if index == ITERS - 1:
            product = exact_dot(product, step)
        elif index == 0:
            product = step
            gram = exact_dot(exact_dot(gram, step), step)
        else:
            both = exact_dot(jnp.concatenate([gram, product], axis=0), step)
            product = both[V:]
            gram = exact_dot(both[:V], step)
        between(index)
    return product * inverse


def coded(total):
    peak = jnp.maximum(jnp.max(jnp.abs(total), axis=0, keepdims=True), 1e-33)
    codes = jnp.round(total * (CODE_MAX / peak)).astype(jnp.int32).astype(jnp.int16)
    return codes, jnp.broadcast_to(peak * (1.0 / CODE_MAX), (8, V))


def decoded(codes, scale):
    return codes.astype(jnp.int32).astype(jnp.float32) * scale


def applied(block, packed):
    matrix = unpack(packed)
    high = matrix.astype(jnp.bfloat16)
    low = (matrix - high.astype(jnp.float32)).astype(jnp.bfloat16)
    return jnp.dot(
        jnp.concatenate([block, block], axis=1),
        jnp.concatenate([high, low], axis=0),
        preferred_element_type=jnp.float32,
    ).astype(jnp.bfloat16)


def communicate(
    grads, params, ortho, held_params,
    mine, theirs, codes, scales, got_codes, got_scales,
    tail_codes, tail_scales, got_tail, got_tail_scales,
    x, p, total, sums, from_x, from_z,
    mine_sems, their_sems, their_send, code_sems, scale_sems, code_send, scale_send,
    tail_sem, tail_scale_sem, tail_send, tail_scale_send, tailx_sem, tailx_send, tails_sem, tails_send,
    gx_sems, gx_send, gz_sems, gz_send, x_sems, x_send, p_sems, p_send, tailp_sem, params_sem,
    *, count, rows,
):
    piece = rows // TAIL_OWNERS
    me = lax.axis_index("dp")
    shard = lax.axis_index("shard")
    core = lax.rem(me, 2)
    chip = me // 2
    sibling = me + 1 - 2 * core
    tail_block = N_DP + core
    tail_other = N_DP + 1 - core

    def chip_at(offset, sign=1):
        z = lax.rem(chip // 4 + offset // 4, 2)
        y = lax.rem(lax.rem(chip, 4) + 4 + sign * (offset % 4), 4)
        return 4 * z + y

    def to(offset):
        return 2 * chip_at(offset) + core

    def source(offset):
        return 2 * chip_at(offset, -1) + core

    def rows_of(block):
        return pl.ds(block * rows, rows)

    def x_peer(step):
        return shard - lax.rem(shard, 4) + lax.rem(lax.rem(shard, 4) + step, 4)

    def z_peer(step):
        return lax.rem(shard // 4 + step, 4) * 4 + lax.rem(shard, 4)

    def remote(src, dst, send_sem, recv_sem, **device):
        pltpu.make_async_remote_copy(
            src_ref=src, dst_ref=dst, send_sem=send_sem, recv_sem=recv_sem,
            device_id=device, device_id_type=MESH,
        ).start()

    def finished(ref, sem):
        pltpu.make_async_copy(ref, ref, sem).wait()

    order = (6, 2, 5, 7, 4, 1, 3)

    barrier = pltpu.get_barrier_semaphore()
    for offset in range(1, CHIPS):
        pl.semaphore_signal(barrier, inc=1, device_id={"dp": to(offset)}, device_id_type=MESH)
    pl.semaphore_signal(barrier, inc=1, device_id={"dp": sibling}, device_id_type=MESH)
    for step in range(1, 4):
        pl.semaphore_signal(barrier, inc=1, device_id={"shard": x_peer(step)}, device_id_type=MESH)
        pl.semaphore_signal(barrier, inc=1, device_id={"shard": z_peer(step)}, device_id_type=MESH)

    pltpu.make_async_copy(grads.at[rows_of(tail_block)], mine.at[CHIPS], mine_sems.at[CHIPS]).start()
    for offset in order + (0,):
        pltpu.make_async_copy(
            grads.at[rows_of(to(offset))], mine.at[offset], mine_sems.at[offset]
        ).start()
    pl.semaphore_wait(barrier, CHIPS + 6)
    remote(grads.at[rows_of(tail_other)], theirs.at[CHIPS], their_send, their_sems.at[CHIPS], dp=sibling)
    for offset in order + (0,):
        remote(
            grads.at[rows_of(to(offset) + 1 - 2 * core)],
            theirs.at[offset],
            their_send,
            their_sems.at[offset],
            dp=sibling,
        )
    keep_params = pltpu.make_async_copy(params, held_params, params_sem)
    keep_params.start()

    def pair_sum(slot):
        finished(mine.at[slot], mine_sems.at[slot])
        finished(theirs.at[slot], their_sems.at[slot])
        return mine[slot].astype(jnp.float32) + theirs[slot].astype(jnp.float32)

    pair = pair_sum(CHIPS)
    packed, scale = coded(pair)
    tail_codes[...] = packed
    tail_scales[...] = scale
    for offset in order:
        peer = chip_at(offset)

        @pl.when(peer < TAIL_OWNERS)
        def _():
            remote(
                tail_codes.at[pl.ds(peer * piece, piece)], got_tail.at[offset], tail_send, tail_sem,
                dp=2 * peer + core,
            )
            remote(tail_scales, got_tail_scales.at[offset], tail_scale_send, tail_scale_sem, dp=2 * peer + core)

    def send_codes(offset):
        packed, scale = coded(pair_sum(offset))
        codes[offset] = packed
        scales[offset] = scale
        remote(codes.at[offset], got_codes.at[offset], code_send, code_sems.at[offset], dp=to(offset))
        remote(scales.at[offset], got_scales.at[offset], scale_send, scale_sems.at[offset], dp=to(offset))

    for offset in order[:4]:
        send_codes(offset)

    tail_rows = pl.ds(tail_block * rows + chip * piece, piece)

    @pl.when(chip < TAIL_OWNERS)
    def _():
        here = pl.ds(pl.multiple_of(chip * piece, piece), piece)
        summed = mine[CHIPS, here].astype(jnp.float32) + theirs[CHIPS, here].astype(jnp.float32)
        finished(got_tail.at[pl.ds(1, CHIPS - 1)], tail_sem)
        finished(got_tail_scales.at[pl.ds(1, CHIPS - 1)], tail_scale_sem)
        for offset in range(1, CHIPS):
            summed = summed + decoded(got_tail[offset], got_tail_scales[offset, 0:1])
        x[tail_rows] = summed.astype(jnp.bfloat16)
        for offset in order:
            remote(x.at[tail_rows], x.at[tail_rows], tailx_send, tailx_sem, dp=to(offset))

    for offset in order[4:]:
        send_codes(offset)
    total[...] = pair_sum(0)

    @pl.when(chip < TAIL_OWNERS)
    def _():
        finished(got_tail.at[pl.ds(0, TAIL_OWNERS - 1)], tailx_sem)

    @pl.when(chip >= TAIL_OWNERS)
    def _():
        finished(got_tail.at[pl.ds(0, TAIL_OWNERS)], tailx_sem)

    remote(x.at[rows_of(tail_block)], x.at[rows_of(tail_block)], tails_send, tails_sem, dp=sibling)

    def start_x(which, gram):
        sums[which, 0] = pack(gram)
        for step in (2, 1, 3):
            remote(
                sums.at[which, 0], from_x.at[which, step - 1], gx_send.at[which], gx_sems.at[which],
                shard=x_peer(step),
            )

    def start_z(which):
        finished(from_x.at[which], gx_sems.at[which])
        sums[which, 1] = sums[which, 0] + from_x[which, 0] + from_x[which, 1] + from_x[which, 2]
        for step in (2, 1, 3):
            remote(
                sums.at[which, 1], from_z.at[which, step - 1], gz_send.at[which], gz_sems.at[which],
                shard=z_peer(step),
            )

    def total_gram(which):
        finished(from_z.at[which], gz_sems.at[which])
        return unpack(sums[which, 1] + from_z[which, 0] + from_z[which, 1] + from_z[which, 2])

    start_x(0, gram_of(x[rows_of(tail_block)]))

    for offset in order:
        finished(got_codes.at[offset], code_sems.at[offset])
        finished(got_scales.at[offset], scale_sems.at[offset])
        total[...] = total[...] + decoded(got_codes[offset], got_scales[offset, 0:1])
    here = x.at[rows_of(me)]
    x[rows_of(me)] = total[...].astype(jnp.bfloat16)
    start_x(1, gram_of(x[rows_of(me)]))
    start_z(0)

    for offset in (2, 1, 3):
        remote(here, here, x_send, x_sems.at[offset], dp=to(offset))
    remote(here, here, x_send, x_sems.at[0], dp=sibling)
    start_z(1)
    remote(here, here, x_send, x_sems.at[4], dp=to(4))

    def pass_x(offset):
        place = x.at[rows_of(source(offset))]
        finished(place, x_sems.at[offset])
        remote(place, place, x_send, x_sems.at[CHIPS + offset], dp=sibling)
        if offset == 4:
            for step in (2, 1, 3):
                remote(place, place, x_send, x_sems.at[4 + step], dp=to(step))

    def between_tail(index):
        for offset in ((), (1,), (3,), (2,), (4,))[index]:
            pass_x(offset)

    p[tail_block] = pack(polynomial_of(total_gram(0), between_tail))
    remote(p.at[tail_block], p.at[tail_block], p_send, tailp_sem, dp=sibling)
    ortho[rows_of(tail_block)] = applied(x[rows_of(tail_block)], p[tail_block])

    def between_own(index):
        for offset in ((), (), (5,), (7,), (6,))[index]:
            pass_x(offset)

    p[me] = pack(polynomial_of(total_gram(1), between_own))
    for offset in order:
        remote(p.at[me], p.at[me], p_send, p_sems.at[offset], dp=to(offset))
    remote(p.at[me], p.at[me], p_send, p_sems.at[0], dp=sibling)

    def apply_at(block):
        ortho[rows_of(block)] = applied(x[rows_of(block)], p[block])

    apply_at(me)
    finished(x.at[rows_of(tail_other)], tails_sem)
    finished(p.at[tail_other], tailp_sem)
    apply_at(tail_other)
    finished(x.at[rows_of(sibling)], x_sems.at[0])
    finished(p.at[sibling], p_sems.at[0])
    apply_at(sibling)

    for offset in (4, 1, 3, 5, 7, 2, 6):
        place = p.at[source(offset)]
        finished(place, p_sems.at[offset])
        remote(place, place, p_send, p_sems.at[CHIPS + offset], dp=sibling)
        apply_at(source(offset))
    for offset in (4, 1, 3, 5, 7, 2, 6):
        other = source(offset) + 1 - 2 * core
        finished(x.at[rows_of(other)], x_sems.at[CHIPS + offset])
        finished(p.at[other], p_sems.at[CHIPS + offset])
        apply_at(other)

    keep_params.wait()
    finished(theirs, their_send)
    finished(got_codes.at[pl.ds(1, CHIPS - 1)], code_send)
    finished(got_scales.at[pl.ds(1, CHIPS - 1)], scale_send)

    @pl.when(chip < TAIL_OWNERS)
    def _():
        finished(got_tail.at[pl.ds(0, TAIL_OWNERS - 1)], tail_send)
        finished(got_tail_scales.at[pl.ds(0, TAIL_OWNERS - 1)], tail_scale_send)
        finished(got_tail.at[pl.ds(0, CHIPS - 1)], tailx_send)

    @pl.when(chip >= TAIL_OWNERS)
    def _():
        finished(got_tail.at[pl.ds(0, TAIL_OWNERS)], tail_send)
        finished(got_tail_scales.at[pl.ds(0, TAIL_OWNERS)], tail_scale_send)

    finished(x.at[rows_of(tail_block)], tails_send)
    for which in range(2):
        finished(from_x.at[which], gx_send.at[which])
        finished(from_z.at[which], gz_send.at[which])
    finished(x.at[pl.ds(0, 15 * rows)], x_send)
    finished(p.at[pl.ds(0, 16)], p_send)


def exchange(grads, params, count, rows):
    piece = rows // TAIL_OWNERS
    dma = pltpu.SemaphoreType.DMA
    vmem = pltpu.VMEM
    return pl.pallas_call(
        functools.partial(communicate, count=count, rows=rows),
        out_shape=(
            jax.ShapeDtypeStruct((count * rows, V), jnp.bfloat16),
            jax.ShapeDtypeStruct((count * rows, V), jnp.float32),
        ),
        in_specs=[pl.BlockSpec(memory_space=pltpu.HBM)] * 2,
        out_specs=(pl.BlockSpec(memory_space=vmem), pl.BlockSpec(memory_space=vmem)),
        scratch_shapes=[
            vmem((CHIPS + 1, rows, V), jnp.bfloat16),
            vmem((CHIPS + 1, rows, V), jnp.bfloat16),
            vmem((CHIPS, rows, V), jnp.int16),
            vmem((CHIPS, 8, V), jnp.float32),
            vmem((CHIPS, rows, V), jnp.int16),
            vmem((CHIPS, 8, V), jnp.float32),
            vmem((rows, V), jnp.int16),
            vmem((8, V), jnp.float32),
            vmem((CHIPS, piece, V), jnp.int16),
            vmem((CHIPS, 8, V), jnp.float32),
            vmem((count * rows, V), jnp.bfloat16),
            vmem((count, PACKED, V), jnp.float32),
            vmem((rows, V), jnp.float32),
            vmem((2, 2, PACKED, V), jnp.float32),
            vmem((2, 3, PACKED, V), jnp.float32),
            vmem((2, 3, PACKED, V), jnp.float32),
            dma((CHIPS + 1,)), dma((CHIPS + 1,)), dma, dma((CHIPS,)), dma((CHIPS,)), dma, dma,
            dma, dma, dma, dma, dma, dma, dma, dma,
            dma((2,)), dma((2,)), dma((2,)), dma((2,)),
            dma((2 * CHIPS,)), dma, dma((2 * CHIPS,)), dma, dma, dma,
        ],
        compiler_params=pltpu.CompilerParams(
            collective_id=0, has_side_effects=True, vmem_limit_bytes=40 * 2**20
        ),
    )(grads, params)


def finish(table, ortho, params, new_params, update, new_held, update_held, sems):
    count = ortho.shape[0]

    def one(j, carry):
        head = table[j]
        scaled = 0.2 * math.sqrt(max(D, V)) * ortho[j].astype(jnp.float32)
        old = params[head]
        new_held[j] = old - learning_rate * (scaled + decay_rate * old)
        update_held[j] = scaled.astype(jnp.bfloat16)
        pltpu.make_async_copy(new_held.at[j], new_params.at[head], sems.at[0]).start()
        pltpu.make_async_copy(update_held.at[j], update.at[head], sems.at[1]).start()
        return carry

    lax.fori_loop(0, count, one, 0)
    pltpu.make_async_copy(new_held, new_params, sems.at[0]).wait()
    pltpu.make_async_copy(update_held, update, sems.at[1]).wait()


def apply(table, ortho, params):
    vmem = pltpu.VMEM
    return pl.pallas_call(
        finish,
        in_specs=[
            pl.BlockSpec(memory_space=pltpu.SMEM),
            pl.BlockSpec(memory_space=vmem),
            pl.BlockSpec(memory_space=vmem),
        ],
        out_specs=(pl.BlockSpec(memory_space=pltpu.HBM), pl.BlockSpec(memory_space=pltpu.HBM)),
        out_shape=(
            jax.ShapeDtypeStruct(params.shape, jnp.float32),
            jax.ShapeDtypeStruct(params.shape, jnp.bfloat16),
        ),
        scratch_shapes=[
            vmem(params.shape, jnp.float32),
            vmem(params.shape, jnp.bfloat16),
            pltpu.SemaphoreType.DMA((2,)),
        ],
        compiler_params=pltpu.CompilerParams(vmem_limit_bytes=32 * 2**20),
    )(table, ortho, params)


def per_device(grads, params, table):
    count, rows, width = params.shape
    flat = (count * rows, width)
    ortho, held = exchange(pltpu.with_memory_space_constraint(grads.reshape(flat), pltpu.HBM), pltpu.with_memory_space_constraint(params.reshape(flat), pltpu.HBM), count, rows)
    return apply(table, ortho.reshape(params.shape), held.reshape(params.shape))


def solution(mesh):
    return jax.shard_map(
        per_device,
        mesh=mesh,
        in_specs=(P("dp", None, "shard", None), P(None, "shard", None), P()),
        out_specs=(P(None, "shard", None), P(None, "shard", None)),
        check_vma=False,
    )
```

```python
import functools
import math

import jax
import jax.numpy as jnp
from jax import lax
from jax.experimental import pallas as pl
from jax.experimental.pallas import tpu as pltpu
from jax.sharding import PartitionSpec as P

D = 7168
V = 128
HALF = V // 2
PACKED = HALF + 8
ITERS = 5
N_DP = 16
CHIPS = 8
TAIL_OWNERS = 7
CODE_MAX = 32767.0

quintic_one = 3.4445
quintic_two = -4.775
quintic_three = 2.0315
epsilon = 1e-07
learning_rate = 0.02
decay_rate = 0.1

MESH = pl.DeviceIdType.MESH
HIGHEST = lax.Precision.HIGHEST


def exact_dot(left, right):
    return jnp.dot(left, right, precision=HIGHEST, preferred_element_type=jnp.float32)


def places(rows):
    return (
        lax.broadcasted_iota(jnp.int32, (rows, V), 0),
        lax.broadcasted_iota(jnp.int32, (rows, V), 1),
    )


def gram_of(rows):
    return lax.dot_general(
        rows, rows, (((0,), (0,)), ((), ())), preferred_element_type=jnp.float32
    )


def pack(matrix):
    row, col = places(HALF)
    corner = pltpu.roll(matrix[HALF:], HALF, 1)
    body = jnp.where((col < HALF) & (row > col), corner, matrix[:HALF])
    diagonal = jnp.sum(jnp.where(row == col, corner, 0.0), axis=0, keepdims=True)
    return jnp.concatenate([body, jnp.broadcast_to(diagonal, (8, V))], axis=0)


def unpack(packed):
    row, col = places(HALF)
    body, diagonal = packed[:HALF], packed[HALF:HALF + 1]
    turned = jnp.concatenate([body, jnp.zeros_like(body)], axis=0).T
    top = jnp.where((col < HALF) & (row > col), turned[:HALF], body)
    corner = jnp.where(row > col, body, jnp.where(row < col, turned[:HALF], diagonal))
    bottom = jnp.where(col < HALF, turned[HALF:], pltpu.roll(corner, HALF, 1))
    return jnp.concatenate([top, bottom], axis=0)


def polynomial_of(total_gram, between):
    row, col = places(V)
    eye = (row == col).astype(jnp.float32)
    square = jnp.sum(jnp.sum(total_gram * eye, axis=1, keepdims=True), axis=0, keepdims=True)
    inverse = 1.0 / (jnp.sqrt(square) + epsilon)
    gram = (total_gram * inverse) * inverse
    product = None
    for index in range(ITERS):
        step = quintic_one * eye + quintic_two * gram + quintic_three * exact_dot(gram, gram)
        if index == ITERS - 1:
            product = exact_dot(product, step)
        elif index == 0:
            product = step
            gram = exact_dot(exact_dot(gram, step), step)
        else:
            both = exact_dot(jnp.concatenate([gram, product], axis=0), step)
            product = both[V:]
            gram = exact_dot(both[:V], step)
        between(index)
    return product * inverse


def coded(total):
    peak = jnp.maximum(jnp.max(jnp.abs(total), axis=0, keepdims=True), 1e-33)
    codes = jnp.round(total * (CODE_MAX / peak)).astype(jnp.int32).astype(jnp.int16)
    return codes, jnp.broadcast_to(peak * (1.0 / CODE_MAX), (8, V))


def decoded(codes, scale):
    return codes.astype(jnp.int32).astype(jnp.float32) * scale


def applied(block, packed):
    matrix = unpack(packed)
    high = matrix.astype(jnp.bfloat16)
    low = (matrix - high.astype(jnp.float32)).astype(jnp.bfloat16)
    return jnp.dot(
        jnp.concatenate([block, block], axis=1),
        jnp.concatenate([high, low], axis=0),
        preferred_element_type=jnp.float32,
    ).astype(jnp.bfloat16)


def communicate(
    grads, params, ortho, held_params,
    mine, theirs, codes, scales, got_codes, got_scales,
    tail_codes, tail_scales, got_tail, got_tail_scales,
    x, p, total, sums, from_x, from_z,
    mine_sems, their_sems, their_send, code_sems, scale_sems, code_send, scale_send,
    tail_sem, tail_scale_sem, tail_send, tail_scale_send, tailx_sem, tailx_send, tails_sem, tails_send,
    gx_sems, gx_send, gz_sems, gz_send, x_sems, z_sems, x_send, p_sems, p_send, tailp_sem, params_sem,
    *, count, rows,
):
    piece = rows // TAIL_OWNERS
    me = lax.axis_index("dp")
    shard = lax.axis_index("shard")
    core = lax.rem(me, 2)
    chip = me // 2
    sibling = me + 1 - 2 * core
    tail_block = N_DP + core
    tail_other = N_DP + 1 - core

    def chip_at(offset, sign=1):
        z = lax.rem(chip // 4 + offset // 4, 2)
        y = lax.rem(lax.rem(chip, 4) + 4 + sign * (offset % 4), 4)
        return 4 * z + y

    def to(offset):
        return 2 * chip_at(offset) + core

    def source(offset):
        return 2 * chip_at(offset, -1) + core

    def rows_of(block):
        return pl.ds(block * rows, rows)

    def x_peer(step):
        return shard - lax.rem(shard, 4) + lax.rem(lax.rem(shard, 4) + step, 4)

    def z_peer(step):
        return lax.rem(shard // 4 + step, 4) * 4 + lax.rem(shard, 4)

    def remote(src, dst, send_sem, recv_sem, **device):
        pltpu.make_async_remote_copy(
            src_ref=src, dst_ref=dst, send_sem=send_sem, recv_sem=recv_sem,
            device_id=device, device_id_type=MESH,
        ).start()

    def finished(ref, sem):
        pltpu.make_async_copy(ref, ref, sem).wait()

    order = (6, 2, 5, 7, 4, 1, 3)

    barrier = pltpu.get_barrier_semaphore()
    for offset in range(1, CHIPS):
        pl.semaphore_signal(barrier, inc=1, device_id={"dp": to(offset)}, device_id_type=MESH)
    pl.semaphore_signal(barrier, inc=1, device_id={"dp": sibling}, device_id_type=MESH)
    for step in range(1, 4):
        pl.semaphore_signal(barrier, inc=1, device_id={"shard": x_peer(step)}, device_id_type=MESH)
        pl.semaphore_signal(barrier, inc=1, device_id={"shard": z_peer(step)}, device_id_type=MESH)

    pltpu.make_async_copy(grads.at[rows_of(tail_block)], mine.at[CHIPS], mine_sems.at[CHIPS]).start()
    for offset in order + (0,):
        pltpu.make_async_copy(
            grads.at[rows_of(to(offset))], mine.at[offset], mine_sems.at[offset]
        ).start()
    pl.semaphore_wait(barrier, CHIPS + 6)
    remote(grads.at[rows_of(tail_other)], theirs.at[CHIPS], their_send, their_sems.at[CHIPS], dp=sibling)
    for offset in order + (0,):
        remote(
            grads.at[rows_of(to(offset) + 1 - 2 * core)],
            theirs.at[offset],
            their_send,
            their_sems.at[offset],
            dp=sibling,
        )
    keep_params = pltpu.make_async_copy(params, held_params, params_sem)
    keep_params.start()

    def pair_sum(slot):
        finished(mine.at[slot], mine_sems.at[slot])
        finished(theirs.at[slot], their_sems.at[slot])
        return mine[slot].astype(jnp.float32) + theirs[slot].astype(jnp.float32)

    pair = pair_sum(CHIPS)
    packed, scale = coded(pair)
    tail_codes[...] = packed
    tail_scales[...] = scale
    for offset in order:
        peer = chip_at(offset)

        @pl.when(peer < TAIL_OWNERS)
        def _():
            remote(
                tail_codes.at[pl.ds(peer * piece, piece)], got_tail.at[offset], tail_send, tail_sem,
                dp=2 * peer + core,
            )
            remote(tail_scales, got_tail_scales.at[offset], tail_scale_send, tail_scale_sem, dp=2 * peer + core)

    halves = (pl.ds(0, rows // 2), pl.ds(rows // 2, rows // 2))

    def send_codes(half, offset):
        remote(
            codes.at[offset, halves[half]], got_codes.at[offset, halves[half]], code_send,
            code_sems.at[half, offset], dp=to(offset),
        )

    for offset in order:
        packed, scale = coded(pair_sum(offset))
        codes[offset] = packed
        scales[offset] = scale
        remote(scales.at[offset], got_scales.at[offset], scale_send, scale_sems.at[offset], dp=to(offset))
        send_codes(0, offset)

    tail_rows = pl.ds(tail_block * rows + chip * piece, piece)

    @pl.when(chip < TAIL_OWNERS)
    def _():
        here = pl.ds(pl.multiple_of(chip * piece, piece), piece)
        summed = mine[CHIPS, here].astype(jnp.float32) + theirs[CHIPS, here].astype(jnp.float32)
        finished(got_tail.at[pl.ds(1, CHIPS - 1)], tail_sem)
        finished(got_tail_scales.at[pl.ds(1, CHIPS - 1)], tail_scale_sem)
        for offset in range(1, CHIPS):
            summed = summed + decoded(got_tail[offset], got_tail_scales[offset, 0:1])
        x[tail_rows] = summed.astype(jnp.bfloat16)
        for offset in order:
            remote(x.at[tail_rows], x.at[tail_rows], tailx_send, tailx_sem, dp=to(offset))

    for offset in order:
        send_codes(1, offset)
    total[...] = pair_sum(0)

    def start_x(which, gram):
        sums[which, 0] = pack(gram)
        for step in (2, 1, 3):
            remote(
                sums.at[which, 0], from_x.at[which, step - 1], gx_send.at[which], gx_sems.at[which],
                shard=x_peer(step),
            )

    def start_z(which):
        finished(from_x.at[which], gx_sems.at[which])
        sums[which, 1] = sums[which, 0] + from_x[which, 0] + from_x[which, 1] + from_x[which, 2]
        for step in (2, 1, 3):
            remote(
                sums.at[which, 1], from_z.at[which, step - 1], gz_send.at[which], gz_sems.at[which],
                shard=z_peer(step),
            )

    def total_gram(which):
        finished(from_z.at[which], gz_sems.at[which])
        return unpack(sums[which, 1] + from_z[which, 0] + from_z[which, 1] + from_z[which, 2])

    def own_half(half):
        here = halves[half]
        for offset in order:
            finished(got_codes.at[offset, here], code_sems.at[half, offset])
            if half == 0:
                finished(got_scales.at[offset], scale_sems.at[offset])
            total[here] = total[here] + decoded(got_codes[offset, here], got_scales[offset, 0:1])
        summed = total[here].astype(jnp.bfloat16)
        x[pl.ds(me * rows + half * (rows // 2), rows // 2)] = summed
        return gram_of(summed)

    def spread_half(half):
        place = x.at[pl.ds(me * rows + half * (rows // 2), rows // 2)]
        remote(place, place, x_send, z_sems.at[half], dp=to(4))
        for offset in (2, 1, 3):
            remote(place, place, x_send, x_sems.at[offset], dp=to(offset))
        remote(place, place, x_send, x_sems.at[0], dp=sibling)

    def pass_half(half):
        place = x.at[pl.ds(source(4) * rows + half * (rows // 2), rows // 2)]
        finished(place, z_sems.at[half])
        for step in (2, 1, 3):
            remote(place, place, x_send, x_sems.at[4 + step], dp=to(step))

    def pass_x(offset):
        place = x.at[rows_of(source(offset))]
        if offset != 4:
            finished(place, x_sems.at[offset])
        remote(place, place, x_send, x_sems.at[CHIPS + offset], dp=sibling)

    first_gram = own_half(0)
    spread_half(0)

    @pl.when(chip < TAIL_OWNERS)
    def _():
        finished(got_tail.at[pl.ds(0, TAIL_OWNERS - 1)], tailx_sem)

    @pl.when(chip >= TAIL_OWNERS)
    def _():
        finished(got_tail.at[pl.ds(0, TAIL_OWNERS)], tailx_sem)

    remote(x.at[rows_of(tail_block)], x.at[rows_of(tail_block)], tails_send, tails_sem, dp=sibling)

    start_x(0, gram_of(x[rows_of(tail_block)]))
    start_z(0)

    start_x(1, own_half(1) + first_gram)
    spread_half(1)
    pass_half(0)
    start_z(1)
    pass_half(1)

    def between_tail(index):
        for offset in ((), (1,), (3,), (2,), (4,))[index]:
            pass_x(offset)

    p[tail_block] = pack(polynomial_of(total_gram(0), between_tail))
    remote(p.at[tail_block], p.at[tail_block], p_send, tailp_sem, dp=sibling)
    ortho[rows_of(tail_block)] = applied(x[rows_of(tail_block)], p[tail_block])

    p[me] = pack(polynomial_of(total_gram(1), lambda index: None))
    for offset in order:
        remote(p.at[me], p.at[me], p_send, p_sems.at[offset], dp=to(offset))
    remote(p.at[me], p.at[me], p_send, p_sems.at[0], dp=sibling)

    def apply_at(block):
        ortho[rows_of(block)] = applied(x[rows_of(block)], p[block])

    apply_at(me)
    for offset in (5, 7, 6):
        pass_x(offset)
    finished(x.at[rows_of(tail_other)], tails_sem)
    finished(p.at[tail_other], tailp_sem)
    apply_at(tail_other)
    finished(x.at[rows_of(sibling)], x_sems.at[0])
    finished(p.at[sibling], p_sems.at[0])
    apply_at(sibling)

    for offset in (4, 1, 3, 5, 7, 2, 6):
        place = p.at[source(offset)]
        finished(place, p_sems.at[offset])
        remote(place, place, p_send, p_sems.at[CHIPS + offset], dp=sibling)
        apply_at(source(offset))
    for offset in (4, 1, 3, 5, 7, 2, 6):
        other = source(offset) + 1 - 2 * core
        finished(x.at[rows_of(other)], x_sems.at[CHIPS + offset])
        finished(p.at[other], p_sems.at[CHIPS + offset])
        apply_at(other)

    keep_params.wait()
    finished(theirs, their_send)
    finished(got_codes.at[pl.ds(1, CHIPS - 1)], code_send)
    finished(got_scales.at[pl.ds(1, CHIPS - 1)], scale_send)

    @pl.when(chip < TAIL_OWNERS)
    def _():
        finished(got_tail.at[pl.ds(0, TAIL_OWNERS - 1)], tail_send)
        finished(got_tail_scales.at[pl.ds(0, TAIL_OWNERS - 1)], tail_scale_send)
        finished(got_tail.at[pl.ds(0, CHIPS - 1)], tailx_send)

    @pl.when(chip >= TAIL_OWNERS)
    def _():
        finished(got_tail.at[pl.ds(0, TAIL_OWNERS)], tail_send)
        finished(got_tail_scales.at[pl.ds(0, TAIL_OWNERS)], tail_scale_send)

    finished(x.at[rows_of(tail_block)], tails_send)
    for which in range(2):
        finished(from_x.at[which], gx_send.at[which])
        finished(from_z.at[which], gz_send.at[which])
    finished(x.at[pl.ds(0, 15 * rows)], x_send)
    finished(p.at[pl.ds(0, 16)], p_send)


def exchange(grads, params, count, rows):
    piece = rows // TAIL_OWNERS
    dma = pltpu.SemaphoreType.DMA
    vmem = pltpu.VMEM
    return pl.pallas_call(
        functools.partial(communicate, count=count, rows=rows),
        out_shape=(
            jax.ShapeDtypeStruct((count * rows, V), jnp.bfloat16),
            jax.ShapeDtypeStruct((count * rows, V), jnp.float32),
        ),
        in_specs=[pl.BlockSpec(memory_space=pltpu.HBM)] * 2,
        out_specs=(pl.BlockSpec(memory_space=vmem), pl.BlockSpec(memory_space=vmem)),
        scratch_shapes=[
            vmem((CHIPS + 1, rows, V), jnp.bfloat16),
            vmem((CHIPS + 1, rows, V), jnp.bfloat16),
            vmem((CHIPS, rows, V), jnp.int16),
            vmem((CHIPS, 8, V), jnp.float32),
            vmem((CHIPS, rows, V), jnp.int16),
            vmem((CHIPS, 8, V), jnp.float32),
            vmem((rows, V), jnp.int16),
            vmem((8, V), jnp.float32),
            vmem((CHIPS, piece, V), jnp.int16),
            vmem((CHIPS, 8, V), jnp.float32),
            vmem((count * rows, V), jnp.bfloat16),
            vmem((count, PACKED, V), jnp.float32),
            vmem((rows, V), jnp.float32),
            vmem((2, 2, PACKED, V), jnp.float32),
            vmem((2, 3, PACKED, V), jnp.float32),
            vmem((2, 3, PACKED, V), jnp.float32),
            dma((CHIPS + 1,)), dma((CHIPS + 1,)), dma, dma((2, CHIPS)), dma((CHIPS,)), dma, dma,
            dma, dma, dma, dma, dma, dma, dma, dma,
            dma((2,)), dma((2,)), dma((2,)), dma((2,)),
            dma((2 * CHIPS,)), dma((2,)), dma, dma((2 * CHIPS,)), dma, dma, dma,
        ],
        compiler_params=pltpu.CompilerParams(
            collective_id=0, has_side_effects=True, vmem_limit_bytes=40 * 2**20
        ),
    )(grads, params)


def finish(table, ortho, params, new_params, update, new_held, update_held, sems):
    count = ortho.shape[0]

    def one(j, carry):
        head = table[j]
        scaled = 0.2 * math.sqrt(max(D, V)) * ortho[j].astype(jnp.float32)
        old = params[head]
        new_held[j] = old - learning_rate * (scaled + decay_rate * old)
        update_held[j] = scaled.astype(jnp.bfloat16)
        pltpu.make_async_copy(new_held.at[j], new_params.at[head], sems.at[0]).start()
        pltpu.make_async_copy(update_held.at[j], update.at[head], sems.at[1]).start()
        return carry

    lax.fori_loop(0, count, one, 0)
    pltpu.make_async_copy(new_held, new_params, sems.at[0]).wait()
    pltpu.make_async_copy(update_held, update, sems.at[1]).wait()


def apply(table, ortho, params):
    vmem = pltpu.VMEM
    return pl.pallas_call(
        finish,
        in_specs=[
            pl.BlockSpec(memory_space=pltpu.SMEM),
            pl.BlockSpec(memory_space=vmem),
            pl.BlockSpec(memory_space=vmem),
        ],
        out_specs=(pl.BlockSpec(memory_space=pltpu.HBM), pl.BlockSpec(memory_space=pltpu.HBM)),
        out_shape=(
            jax.ShapeDtypeStruct(params.shape, jnp.float32),
            jax.ShapeDtypeStruct(params.shape, jnp.bfloat16),
        ),
        scratch_shapes=[
            vmem(params.shape, jnp.float32),
            vmem(params.shape, jnp.bfloat16),
            pltpu.SemaphoreType.DMA((2,)),
        ],
        compiler_params=pltpu.CompilerParams(vmem_limit_bytes=32 * 2**20),
    )(table, ortho, params)


def per_device(grads, params, table):
    count, rows, width = params.shape
    flat = (count * rows, width)
    ortho, held = exchange(pltpu.with_memory_space_constraint(grads.reshape(flat), pltpu.HBM), pltpu.with_memory_space_constraint(params.reshape(flat), pltpu.HBM), count, rows)
    return apply(table, ortho.reshape(params.shape), held.reshape(params.shape))


def solution(mesh):
    return jax.shard_map(
        per_device,
        mesh=mesh,
        in_specs=(P("dp", None, "shard", None), P(None, "shard", None), P()),
        out_specs=(P(None, "shard", None), P(None, "shard", None)),
        check_vma=False,
    )
```

```python
import functools
import math

import jax
import jax.numpy as jnp
from jax import lax
from jax.experimental import pallas as pl
from jax.experimental.pallas import tpu as pltpu
from jax.sharding import PartitionSpec as P

D = 7168
V = 128
HALF = V // 2
PACKED = HALF + 8
QUARTER = HALF // 4
ITERS = 5
N_DP = 16
CHIPS = 8
TAIL_OWNERS = 7
CODE_MAX = 32767.0

quintic_one = 3.4445
quintic_two = -4.775
quintic_three = 2.0315
epsilon = 1e-07
learning_rate = 0.02
decay_rate = 0.1

MESH = pl.DeviceIdType.MESH


def exact_dot(left, right):
    return jnp.dot(left, right, precision=lax.Precision.HIGHEST, preferred_element_type=jnp.float32)


def places(rows):
    return (
        lax.broadcasted_iota(jnp.int32, (rows, V), 0),
        lax.broadcasted_iota(jnp.int32, (rows, V), 1),
    )


def gram_of(rows):
    return lax.dot_general(
        rows, rows, (((0,), (0,)), ((), ())), preferred_element_type=jnp.float32
    )


def pack(matrix):
    row, col = places(HALF)
    corner = pltpu.roll(matrix[HALF:], HALF, 1)
    body = jnp.where((col < HALF) & (row > col), corner, matrix[:HALF])
    diagonal = jnp.sum(jnp.where(row == col, corner, 0.0), axis=0, keepdims=True)
    return jnp.concatenate([body, jnp.broadcast_to(diagonal, (8, V))], axis=0)


def unpack(packed):
    row, col = places(HALF)
    body, diagonal = packed[:HALF], packed[HALF:HALF + 1]
    turned = jnp.concatenate([body, jnp.zeros_like(body)], axis=0).T
    top = jnp.where((col < HALF) & (row > col), turned[:HALF], body)
    corner = jnp.where(row > col, body, jnp.where(row < col, turned[:HALF], diagonal))
    bottom = jnp.where(col < HALF, turned[HALF:], pltpu.roll(corner, HALF, 1))
    return jnp.concatenate([top, bottom], axis=0)


def polynomial_of(total_gram):
    row, col = places(V)
    eye = (row == col).astype(jnp.float32)
    square = jnp.sum(jnp.sum(total_gram * eye, axis=1, keepdims=True), axis=0, keepdims=True)
    inverse = 1.0 / (jnp.sqrt(square) + epsilon)
    gram = (total_gram * inverse) * inverse
    product = None
    for index in range(ITERS):
        step = quintic_one * eye + quintic_two * gram + quintic_three * exact_dot(gram, gram)
        if index == ITERS - 1:
            product = exact_dot(product, step)
        elif index == 0:
            product = step
            gram = exact_dot(exact_dot(gram, step), step)
        else:
            both = exact_dot(jnp.concatenate([gram, product], axis=0), step)
            product = both[V:]
            gram = exact_dot(both[:V], step)
    return product * inverse


def coded(total):
    peak = jnp.maximum(jnp.max(jnp.abs(total), axis=0, keepdims=True), 1e-33)
    codes = jnp.round(total * (CODE_MAX / peak)).astype(jnp.int32).astype(jnp.int16)
    return codes, jnp.broadcast_to(peak * (1.0 / CODE_MAX), (8, V))


def decoded(codes, scale):
    return codes.astype(jnp.int32).astype(jnp.float32) * scale


def applied(block, packed):
    matrix = unpack(packed)
    high = matrix.astype(jnp.bfloat16)
    low = (matrix - high.astype(jnp.float32)).astype(jnp.bfloat16)
    return jnp.dot(
        jnp.concatenate([block, block], axis=1),
        jnp.concatenate([high, low], axis=0),
        preferred_element_type=jnp.float32,
    ).astype(jnp.bfloat16)


def communicate(
    grads, params, ortho, held_params,
    mine, given, theirs, codes, scales, got_codes, got_scales,
    tail_codes, tail_scales, got_tail, got_tail_scales,
    x, p, total, parts, sums, quarters, from_x, from_z, whole, whole_x, whole_z,
    mine_sems, given_sems, their_sems, their_send, code_sems, scale_sems, code_send, scale_send,
    tail_sem, tail_scale_sem, tail_send, tail_scale_send, tailx_sem, tailx_send, tails_sem, tails_send,
    gx_sem, gx_send, gz_sem, gz_send, gq_sem, gq_send, wx_sem, wx_send, wz_sem, wz_send, x_sems, z_sems, x_send, p_sems, p_send, tailp_sem, params_sem,
    *, count, rows,
):
    piece = rows // TAIL_OWNERS
    me = lax.axis_index("dp")
    shard = lax.axis_index("shard")
    core = lax.rem(me, 2)
    chip = me // 2
    sibling = me + 1 - 2 * core
    tail_block = N_DP + core
    tail_other = N_DP + 1 - core

    def chip_at(offset, sign=1):
        z = lax.rem(chip // 4 + offset // 4, 2)
        y = lax.rem(lax.rem(chip, 4) + 4 + sign * (offset % 4), 4)
        return 4 * z + y

    def to(offset):
        return 2 * chip_at(offset) + core

    def source(offset):
        return 2 * chip_at(offset, -1) + core

    def rows_of(block):
        return pl.ds(block * rows, rows)

    def x_peer(step):
        return shard - lax.rem(shard, 4) + lax.rem(lax.rem(shard, 4) + step, 4)

    def z_peer(step):
        return lax.rem(shard // 4 + step, 4) * 4 + lax.rem(shard, 4)

    def remote(src, dst, send_sem, recv_sem, **device):
        pltpu.make_async_remote_copy(
            src_ref=src, dst_ref=dst, send_sem=send_sem, recv_sem=recv_sem,
            device_id=device, device_id_type=MESH,
        ).start()

    def finished(ref, sem):
        pltpu.make_async_copy(ref, ref, sem).wait()

    order = (6, 2, 5, 7, 4, 1, 3)

    barrier = pltpu.get_barrier_semaphore()
    for offset in range(1, CHIPS):
        pl.semaphore_signal(barrier, inc=1, device_id={"dp": to(offset)}, device_id_type=MESH)
    pl.semaphore_signal(barrier, inc=1, device_id={"dp": sibling}, device_id_type=MESH)
    for step in range(1, 4):
        pl.semaphore_signal(barrier, inc=1, device_id={"shard": x_peer(step)}, device_id_type=MESH)
        pl.semaphore_signal(barrier, inc=1, device_id={"shard": z_peer(step)}, device_id_type=MESH)

    first_slots = ((CHIPS, tail_block, tail_other),) + tuple(
        (offset, to(offset), to(offset) + 1 - 2 * core) for offset in order + (0,)
    )
    for slot, _, block in first_slots:
        pltpu.make_async_copy(grads.at[rows_of(block)], given.at[slot], given_sems.at[slot]).start()
    for slot, block, _ in first_slots:
        pltpu.make_async_copy(grads.at[rows_of(block)], mine.at[slot], mine_sems.at[slot]).start()
    for slot, _, _ in first_slots:
        finished(given.at[slot], given_sems.at[slot])
    pl.semaphore_wait(barrier, CHIPS + 6)
    for slot, _, _ in first_slots:
        remote(given.at[slot], theirs.at[slot], their_send, their_sems.at[slot], dp=sibling)
    keep_params = pltpu.make_async_copy(params, held_params, params_sem)
    keep_params.start()

    def pair_sum(slot):
        finished(mine.at[slot], mine_sems.at[slot])
        finished(theirs.at[slot], their_sems.at[slot])
        return mine[slot].astype(jnp.float32) + theirs[slot].astype(jnp.float32)

    pair = pair_sum(CHIPS)
    packed, scale = coded(pair)
    tail_codes[...] = packed
    tail_scales[...] = scale
    for offset in order:
        peer = chip_at(offset)

        @pl.when(peer < TAIL_OWNERS)
        def _():
            remote(
                tail_codes.at[pl.ds(peer * piece, piece)], got_tail.at[offset], tail_send, tail_sem,
                dp=2 * peer + core,
            )
            remote(tail_scales, got_tail_scales.at[offset], tail_scale_send, tail_scale_sem, dp=2 * peer + core)

    halves = (pl.ds(0, rows // 2), pl.ds(rows // 2, rows // 2))

    def send_codes(half, offset):
        remote(
            codes.at[offset, halves[half]], got_codes.at[offset, halves[half]], code_send,
            code_sems.at[half, offset], dp=to(offset),
        )

    for offset in order:
        packed, scale = coded(pair_sum(offset))
        codes[offset] = packed
        scales[offset] = scale
        remote(scales.at[offset], got_scales.at[offset], scale_send, scale_sems.at[offset], dp=to(offset))
        send_codes(0, offset)

    tail_rows = pl.ds(tail_block * rows + chip * piece, piece)

    @pl.when(chip < TAIL_OWNERS)
    def _():
        here = pl.ds(pl.multiple_of(chip * piece, piece), piece)
        summed = mine[CHIPS, here].astype(jnp.float32) + theirs[CHIPS, here].astype(jnp.float32)
        finished(got_tail.at[pl.ds(1, CHIPS - 1)], tail_sem)
        finished(got_tail_scales.at[pl.ds(1, CHIPS - 1)], tail_scale_sem)
        for offset in range(1, CHIPS):
            summed = summed + decoded(got_tail[offset], got_tail_scales[offset, 0:1])
        x[tail_rows] = summed.astype(jnp.bfloat16)
        for offset in order:
            remote(x.at[tail_rows], x.at[tail_rows], tailx_send, tailx_sem, dp=to(offset))

    for offset in order:
        send_codes(1, offset)
    total[...] = pair_sum(0)

    across = lax.rem(shard, 4)

    def tail_start_x(gram):
        packed = pack(gram)
        for quarter in range(4):
            parts[quarter] = jnp.concatenate(
                [packed[QUARTER * quarter:QUARTER * (quarter + 1)], packed[HALF:]], axis=0
            )
        for step in (2, 1, 3):
            remote(
                parts.at[lax.rem(across + step, 4)], from_x.at[step - 1], gx_send, gx_sem,
                shard=x_peer(step),
            )

    def tail_start_z():
        finished(from_x, gx_sem)
        sums[...] = parts[across] + from_x[0] + from_x[1] + from_x[2]
        for step in (2, 1, 3):
            remote(sums, from_z.at[step - 1], gz_send, gz_sem, shard=z_peer(step))

    def tail_start_quarters():
        finished(from_z, gz_sem)
        quarters[across] = sums[...] + from_z[0] + from_z[1] + from_z[2]
        for step in (2, 1, 3):
            remote(quarters.at[across], quarters.at[across], gq_send, gq_sem, shard=x_peer(step))

    def tail_gram():
        finished(from_x, gq_sem)
        rows_in = [quarters[quarter, :QUARTER] for quarter in range(4)]
        return unpack(jnp.concatenate(rows_in + [quarters[0, QUARTER:]], axis=0))

    def start_x(gram):
        whole[0] = pack(gram)
        for step in (2, 1, 3):
            remote(whole.at[0], whole_x.at[step - 1], wx_send, wx_sem, shard=x_peer(step))

    def start_z():
        finished(whole_x, wx_sem)
        whole[1] = whole[0] + whole_x[0] + whole_x[1] + whole_x[2]
        for step in (2, 1, 3):
            remote(whole.at[1], whole_z.at[step - 1], wz_send, wz_sem, shard=z_peer(step))

    def own_gram():
        finished(whole_z, wz_sem)
        return unpack(whole[1] + whole_z[0] + whole_z[1] + whole_z[2])

    def own_half(half):
        here = halves[half]
        for offset in order:
            finished(got_codes.at[offset, here], code_sems.at[half, offset])
            if half == 0:
                finished(got_scales.at[offset], scale_sems.at[offset])
            total[here] = total[here] + decoded(got_codes[offset, here], got_scales[offset, 0:1])
        summed = total[here].astype(jnp.bfloat16)
        x[pl.ds(me * rows + half * (rows // 2), rows // 2)] = summed
        return gram_of(summed)

    def spread_half(half):
        place = x.at[pl.ds(me * rows + half * (rows // 2), rows // 2)]
        remote(place, place, x_send, z_sems.at[half], dp=to(4))
        for offset in (2, 1, 3):
            remote(place, place, x_send, x_sems.at[offset], dp=to(offset))
        remote(place, place, x_send, x_sems.at[0], dp=sibling)

    def pass_half(half):
        place = x.at[pl.ds(source(4) * rows + half * (rows // 2), rows // 2)]
        finished(place, z_sems.at[half])
        for step in (2, 1, 3):
            remote(place, place, x_send, x_sems.at[4 + step], dp=to(step))

    def pass_x(offset):
        place = x.at[rows_of(source(offset))]
        if offset != 4:
            finished(place, x_sems.at[offset])
        remote(place, place, x_send, x_sems.at[CHIPS + offset], dp=sibling)

    first_gram = own_half(0)
    spread_half(0)

    @pl.when(chip < TAIL_OWNERS)
    def _():
        finished(got_tail.at[pl.ds(0, TAIL_OWNERS - 1)], tailx_sem)

    @pl.when(chip >= TAIL_OWNERS)
    def _():
        finished(got_tail.at[pl.ds(0, TAIL_OWNERS)], tailx_sem)

    remote(x.at[rows_of(tail_block)], x.at[rows_of(tail_block)], tails_send, tails_sem, dp=sibling)

    tail_start_x(gram_of(x[rows_of(tail_block)]))
    tail_start_z()

    start_x(own_half(1) + first_gram)
    spread_half(1)
    pass_half(0)
    start_z()
    pass_half(1)
    pass_x(4)
    tail_start_quarters()
    for offset in (1, 3, 2):
        pass_x(offset)

    def send_matrix(block, matrix):
        p[block] = pack(matrix)
        if block is me:
            for offset in order:
                remote(p.at[me], p.at[me], p_send, p_sems.at[offset], dp=to(offset))
        remote(p.at[block], p.at[block], p_send, p_sems.at[0] if block is me else tailp_sem, dp=sibling)

    send_matrix(me, polynomial_of(own_gram()))
    for offset in (5, 7, 6):
        pass_x(offset)
    send_matrix(tail_block, polynomial_of(tail_gram()))

    def apply_at(*blocks):
        results = [applied(x[rows_of(block)], p[block]) for block in blocks]
        for block, result in zip(blocks, results):
            ortho[rows_of(block)] = result

    def pass_p(offset):
        place = p.at[source(offset)]
        finished(place, p_sems.at[offset])
        remote(place, place, p_send, p_sems.at[CHIPS + offset], dp=sibling)

    def other_of(offset):
        return source(offset) + 1 - 2 * core

    finished(x.at[rows_of(sibling)], x_sems.at[0])
    finished(p.at[sibling], p_sems.at[0])
    for offset in (4, 1, 3):
        pass_p(offset)
    apply_at(me, sibling, source(4), source(1), source(3))
    for offset in (5, 7, 2, 6):
        pass_p(offset)
    finished(x.at[rows_of(tail_other)], tails_sem)
    finished(p.at[tail_other], tailp_sem)
    apply_at(tail_block, tail_other, source(5), source(7), source(2), source(6))
    for offset in (4, 1, 3, 5, 7, 2, 6):
        other = other_of(offset)
        finished(x.at[rows_of(other)], x_sems.at[CHIPS + offset])
        finished(p.at[other], p_sems.at[CHIPS + offset])
    apply_at(*(other_of(offset) for offset in (4, 1, 3, 5, 7, 2, 6)))

    keep_params.wait()
    finished(theirs, their_send)
    finished(got_codes.at[pl.ds(1, CHIPS - 1)], code_send)
    finished(got_scales.at[pl.ds(1, CHIPS - 1)], scale_send)

    @pl.when(chip < TAIL_OWNERS)
    def _():
        finished(got_tail.at[pl.ds(0, TAIL_OWNERS - 1)], tail_send)
        finished(got_tail_scales.at[pl.ds(0, TAIL_OWNERS - 1)], tail_scale_send)
        finished(got_tail.at[pl.ds(0, CHIPS - 1)], tailx_send)

    @pl.when(chip >= TAIL_OWNERS)
    def _():
        finished(got_tail.at[pl.ds(0, TAIL_OWNERS)], tail_send)
        finished(got_tail_scales.at[pl.ds(0, TAIL_OWNERS)], tail_scale_send)

    finished(x.at[rows_of(tail_block)], tails_send)
    finished(from_x, gx_send)
    finished(from_z, gz_send)
    finished(from_x, gq_send)
    finished(whole_x, wx_send)
    finished(whole_z, wz_send)
    finished(x.at[pl.ds(0, 15 * rows)], x_send)
    finished(p.at[pl.ds(0, 16)], p_send)


def exchange(grads, params, count, rows):
    piece = rows // TAIL_OWNERS
    dma = pltpu.SemaphoreType.DMA
    vmem = pltpu.VMEM
    return pl.pallas_call(
        functools.partial(communicate, count=count, rows=rows),
        out_shape=(
            jax.ShapeDtypeStruct((count * rows, V), jnp.bfloat16),
            jax.ShapeDtypeStruct((count * rows, V), jnp.float32),
        ),
        in_specs=[pl.BlockSpec(memory_space=pltpu.HBM)] * 2,
        out_specs=(pl.BlockSpec(memory_space=vmem), pl.BlockSpec(memory_space=vmem)),
        scratch_shapes=[
            vmem((CHIPS + 1, rows, V), jnp.bfloat16),
            vmem((CHIPS + 1, rows, V), jnp.bfloat16),
            vmem((CHIPS + 1, rows, V), jnp.bfloat16),
            vmem((CHIPS, rows, V), jnp.int16),
            vmem((CHIPS, 8, V), jnp.float32),
            vmem((CHIPS, rows, V), jnp.int16),
            vmem((CHIPS, 8, V), jnp.float32),
            vmem((rows, V), jnp.int16),
            vmem((8, V), jnp.float32),
            vmem((CHIPS, piece, V), jnp.int16),
            vmem((CHIPS, 8, V), jnp.float32),
            vmem((count * rows, V), jnp.bfloat16),
            vmem((count, PACKED, V), jnp.float32),
            vmem((rows, V), jnp.float32),
            vmem((4, QUARTER + 8, V), jnp.float32),
            vmem((QUARTER + 8, V), jnp.float32),
            vmem((4, QUARTER + 8, V), jnp.float32),
            vmem((3, QUARTER + 8, V), jnp.float32),
            vmem((3, QUARTER + 8, V), jnp.float32),
            vmem((2, PACKED, V), jnp.float32),
            vmem((3, PACKED, V), jnp.float32),
            vmem((3, PACKED, V), jnp.float32),
            dma((CHIPS + 1,)), dma((CHIPS + 1,)), dma((CHIPS + 1,)), dma, dma((2, CHIPS)), dma((CHIPS,)), dma, dma,
            dma, dma, dma, dma, dma, dma, dma, dma,
            dma, dma, dma, dma, dma, dma, dma, dma, dma, dma,
            dma((2 * CHIPS,)), dma((2,)), dma, dma((2 * CHIPS,)), dma, dma, dma,
        ],
        compiler_params=pltpu.CompilerParams(
            collective_id=0, has_side_effects=True, vmem_limit_bytes=40 * 2**20
        ),
    )(grads, params)


def finish(table, ortho, params, new_params, update, new_held, update_held, sems):
    count = ortho.shape[0]

    def one(j, carry):
        head = table[j]
        scaled = 0.2 * math.sqrt(max(D, V)) * ortho[j].astype(jnp.float32)
        old = params[head]
        new_held[j] = old - learning_rate * (scaled + decay_rate * old)
        update_held[j] = scaled.astype(jnp.bfloat16)
        pltpu.make_async_copy(new_held.at[j], new_params.at[head], sems.at[0]).start()
        pltpu.make_async_copy(update_held.at[j], update.at[head], sems.at[1]).start()
        return carry

    lax.fori_loop(0, count, one, 0)
    pltpu.make_async_copy(new_held, new_params, sems.at[0]).wait()
    pltpu.make_async_copy(update_held, update, sems.at[1]).wait()


def apply(table, ortho, params):
    vmem = pltpu.VMEM
    return pl.pallas_call(
        finish,
        in_specs=[
            pl.BlockSpec(memory_space=pltpu.SMEM),
            pl.BlockSpec(memory_space=vmem),
            pl.BlockSpec(memory_space=vmem),
        ],
        out_specs=(pl.BlockSpec(memory_space=pltpu.HBM), pl.BlockSpec(memory_space=pltpu.HBM)),
        out_shape=(
            jax.ShapeDtypeStruct(params.shape, jnp.float32),
            jax.ShapeDtypeStruct(params.shape, jnp.bfloat16),
        ),
        scratch_shapes=[
            vmem(params.shape, jnp.float32),
            vmem(params.shape, jnp.bfloat16),
            pltpu.SemaphoreType.DMA((2,)),
        ],
        compiler_params=pltpu.CompilerParams(vmem_limit_bytes=32 * 2**20),
    )(table, ortho, params)


def per_device(grads, params, table):
    count, rows, width = params.shape
    flat = (count * rows, width)
    ortho, held = exchange(pltpu.with_memory_space_constraint(grads.reshape(flat), pltpu.HBM), pltpu.with_memory_space_constraint(params.reshape(flat), pltpu.HBM), count, rows)
    return apply(table, ortho.reshape(params.shape), held.reshape(params.shape))


def solution(mesh):
    return jax.shard_map(
        per_device,
        mesh=mesh,
        in_specs=(P("dp", None, "shard", None), P(None, "shard", None), P()),
        out_specs=(P(None, "shard", None), P(None, "shard", None)),
        check_vma=False,
    )
```

```python
import functools
import math

import jax
import jax.numpy as jnp
from jax import lax
from jax.experimental import pallas as pl
from jax.experimental.pallas import tpu as pltpu
from jax.sharding import PartitionSpec as P

D = 7168
V = 128
HALF = V // 2
PACKED = HALF + 8
ITERS = 5
N_DP = 16
CHIPS = 8
TAIL_OWNERS = 7
CODE_MAX = 32767.0

quintic_one = 3.4445
quintic_two = -4.775
quintic_three = 2.0315
epsilon = 1e-07
learning_rate = 0.02
decay_rate = 0.1

MESH = pl.DeviceIdType.MESH


def exact_dot(left, right):
    return jnp.dot(left, right, precision=lax.Precision.HIGHEST, preferred_element_type=jnp.float32)


def places(rows):
    return (
        lax.broadcasted_iota(jnp.int32, (rows, V), 0),
        lax.broadcasted_iota(jnp.int32, (rows, V), 1),
    )


def gram_of(rows):
    return lax.dot_general(
        rows, rows, (((0,), (0,)), ((), ())), preferred_element_type=jnp.float32
    )


def pack(matrix):
    row, col = places(HALF)
    corner = pltpu.roll(matrix[HALF:], HALF, 1)
    body = jnp.where((col < HALF) & (row > col), corner, matrix[:HALF])
    diagonal = jnp.sum(jnp.where(row == col, corner, 0.0), axis=0, keepdims=True)
    return jnp.concatenate([body, jnp.broadcast_to(diagonal, (8, V))], axis=0)


def unpack(packed):
    row, col = places(HALF)
    body, diagonal = packed[:HALF], packed[HALF:HALF + 1]
    turned = jnp.concatenate([body, jnp.zeros_like(body)], axis=0).T
    top = jnp.where((col < HALF) & (row > col), turned[:HALF], body)
    corner = jnp.where(row > col, body, jnp.where(row < col, turned[:HALF], diagonal))
    bottom = jnp.where(col < HALF, turned[HALF:], pltpu.roll(corner, HALF, 1))
    return jnp.concatenate([top, bottom], axis=0)


def polynomial_of(total_gram):
    row, col = places(V)
    eye = (row == col).astype(jnp.float32)
    square = jnp.sum(jnp.sum(total_gram * eye, axis=1, keepdims=True), axis=0, keepdims=True)
    inverse = 1.0 / (jnp.sqrt(square) + epsilon)
    gram = (total_gram * inverse) * inverse
    product = None
    for index in range(ITERS):
        step = quintic_one * eye + quintic_two * gram + quintic_three * exact_dot(gram, gram)
        if index == ITERS - 1:
            product = exact_dot(product, step)
        elif index == 0:
            product = step
            gram = exact_dot(exact_dot(gram, step), step)
        else:
            both = exact_dot(jnp.concatenate([gram, product], axis=0), step)
            product = both[V:]
            gram = exact_dot(both[:V], step)
    return product * inverse


def coded(total):
    peak = jnp.maximum(jnp.max(jnp.abs(total), axis=0, keepdims=True), 1e-33)
    codes = jnp.round(total * (CODE_MAX / peak)).astype(jnp.int32).astype(jnp.int16)
    return codes, jnp.broadcast_to(peak * (1.0 / CODE_MAX), (8, V))


def decoded(codes, scale):
    return codes.astype(jnp.int32).astype(jnp.float32) * scale


def applied(block, packed):
    matrix = unpack(packed)
    high = matrix.astype(jnp.bfloat16)
    low = (matrix - high.astype(jnp.float32)).astype(jnp.bfloat16)
    return jnp.dot(
        jnp.concatenate([block, block], axis=1),
        jnp.concatenate([high, low], axis=0),
        preferred_element_type=jnp.float32,
    ).astype(jnp.bfloat16)


def communicate(
    grads, params, ortho, held_params,
    mine, given, theirs, codes, scales, got_codes, got_scales,
    tail_codes, tail_scales, got_tail, got_tail_scales,
    x, p, total, sums, from_x, from_z,
    mine_sems, given_sems, their_sems, their_send, code_sems, scale_sems, code_send, scale_send,
    tail_sem, tail_scale_sem, tail_send, tail_scale_send, tailx_sem, tailx_send, tails_sem, tails_send,
    gx_sems, gx_send, gz_sems, gz_send, x_sems, z_sems, x_send, p_sems, p_send, tailp_sem, params_sem,
    *, count, rows,
):
    piece = rows // TAIL_OWNERS
    me = lax.axis_index("dp")
    shard = lax.axis_index("shard")
    core = lax.rem(me, 2)
    chip = me // 2
    sibling = me + 1 - 2 * core
    tail_block = N_DP + core
    tail_other = N_DP + 1 - core

    def chip_at(offset, sign=1):
        z = lax.rem(chip // 4 + offset // 4, 2)
        y = lax.rem(lax.rem(chip, 4) + 4 + sign * (offset % 4), 4)
        return 4 * z + y

    def to(offset):
        return 2 * chip_at(offset) + core

    def source(offset):
        return 2 * chip_at(offset, -1) + core

    def rows_of(block):
        return pl.ds(block * rows, rows)

    def x_peer(step):
        return shard - lax.rem(shard, 4) + lax.rem(lax.rem(shard, 4) + step, 4)

    def z_peer(step):
        return lax.rem(shard // 4 + step, 4) * 4 + lax.rem(shard, 4)

    def remote(src, dst, send_sem, recv_sem, **device):
        pltpu.make_async_remote_copy(
            src_ref=src, dst_ref=dst, send_sem=send_sem, recv_sem=recv_sem,
            device_id=device, device_id_type=MESH,
        ).start()

    def finished(ref, sem):
        pltpu.make_async_copy(ref, ref, sem).wait()

    order = (6, 2, 5, 7, 4, 1, 3)

    barrier = pltpu.get_barrier_semaphore()
    for offset in range(1, CHIPS):
        pl.semaphore_signal(barrier, inc=1, device_id={"dp": to(offset)}, device_id_type=MESH)
    pl.semaphore_signal(barrier, inc=1, device_id={"dp": sibling}, device_id_type=MESH)
    for step in range(1, 4):
        pl.semaphore_signal(barrier, inc=1, device_id={"shard": x_peer(step)}, device_id_type=MESH)
        pl.semaphore_signal(barrier, inc=1, device_id={"shard": z_peer(step)}, device_id_type=MESH)

    first_slots = ((CHIPS, tail_block, tail_other),) + tuple(
        (offset, to(offset), to(offset) + 1 - 2 * core) for offset in order + (0,)
    )
    for slot, _, block in first_slots:
        pltpu.make_async_copy(grads.at[rows_of(block)], given.at[slot], given_sems.at[slot]).start()
    for slot, block, _ in first_slots:
        pltpu.make_async_copy(grads.at[rows_of(block)], mine.at[slot], mine_sems.at[slot]).start()
    for slot, _, _ in first_slots:
        finished(given.at[slot], given_sems.at[slot])
    pl.semaphore_wait(barrier, CHIPS + 6)
    for slot, _, _ in first_slots:
        remote(given.at[slot], theirs.at[slot], their_send, their_sems.at[slot], dp=sibling)
    keep_params = pltpu.make_async_copy(params, held_params, params_sem)
    keep_params.start()

    def pair_sum(slot):
        finished(mine.at[slot], mine_sems.at[slot])
        finished(theirs.at[slot], their_sems.at[slot])
        return mine[slot].astype(jnp.float32) + theirs[slot].astype(jnp.float32)

    pair = pair_sum(CHIPS)
    packed, scale = coded(pair)
    tail_codes[...] = packed
    tail_scales[...] = scale
    for offset in order:
        peer = chip_at(offset)

        @pl.when(peer < TAIL_OWNERS)
        def _():
            remote(
                tail_codes.at[pl.ds(peer * piece, piece)], got_tail.at[offset], tail_send, tail_sem,
                dp=2 * peer + core,
            )
            remote(tail_scales, got_tail_scales.at[offset], tail_scale_send, tail_scale_sem, dp=2 * peer + core)

    halves = (pl.ds(0, rows // 2), pl.ds(rows // 2, rows // 2))

    def send_codes(half, offset):
        remote(
            codes.at[offset, halves[half]], got_codes.at[offset, halves[half]], code_send,
            code_sems.at[half, offset], dp=to(offset),
        )

    for offset in order:
        packed, scale = coded(pair_sum(offset))
        codes[offset] = packed
        scales[offset] = scale
        remote(scales.at[offset], got_scales.at[offset], scale_send, scale_sems.at[offset], dp=to(offset))
        send_codes(0, offset)

    for offset in order:
        send_codes(1, offset)

    tail_rows = pl.ds(tail_block * rows + chip * piece, piece)

    @pl.when(chip < TAIL_OWNERS)
    def _():
        here = pl.ds(pl.multiple_of(chip * piece, piece), piece)
        summed = mine[CHIPS, here].astype(jnp.float32) + theirs[CHIPS, here].astype(jnp.float32)
        finished(got_tail.at[pl.ds(1, CHIPS - 1)], tail_sem)
        finished(got_tail_scales.at[pl.ds(1, CHIPS - 1)], tail_scale_sem)
        for offset in range(1, CHIPS):
            summed = summed + decoded(got_tail[offset], got_tail_scales[offset, 0:1])
        x[tail_rows] = summed.astype(jnp.bfloat16)
        for offset in order:
            remote(x.at[tail_rows], x.at[tail_rows], tailx_send, tailx_sem, dp=to(offset))

    total[...] = pair_sum(0)

    def start_x(which, gram):
        sums[which, 0] = pack(gram)
        for step in (2, 1, 3):
            remote(
                sums.at[which, 0], from_x.at[which, step - 1], gx_send.at[which], gx_sems.at[which],
                shard=x_peer(step),
            )

    def start_z(which):
        finished(from_x.at[which], gx_sems.at[which])
        sums[which, 1] = sums[which, 0] + from_x[which, 0] + from_x[which, 1] + from_x[which, 2]
        for step in (2, 1, 3):
            remote(
                sums.at[which, 1], from_z.at[which, step - 1], gz_send.at[which], gz_sems.at[which],
                shard=z_peer(step),
            )

    def total_gram(which):
        finished(from_z.at[which], gz_sems.at[which])
        return unpack(sums[which, 1] + from_z[which, 0] + from_z[which, 1] + from_z[which, 2])

    def own_half(half):
        here = halves[half]
        for offset in order:
            finished(got_codes.at[offset, here], code_sems.at[half, offset])
            if half == 0:
                finished(got_scales.at[offset], scale_sems.at[offset])
            total[here] = total[here] + decoded(got_codes[offset, here], got_scales[offset, 0:1])
        summed = total[here].astype(jnp.bfloat16)
        x[pl.ds(me * rows + half * (rows // 2), rows // 2)] = summed
        return gram_of(summed)

    def spread_half(half):
        place = x.at[pl.ds(me * rows + half * (rows // 2), rows // 2)]
        remote(place, place, x_send, z_sems.at[half], dp=to(4))
        for offset in (2, 1, 3):
            remote(place, place, x_send, x_sems.at[offset], dp=to(offset))
        remote(place, place, x_send, x_sems.at[0], dp=sibling)

    def pass_half(half):
        place = x.at[pl.ds(source(4) * rows + half * (rows // 2), rows // 2)]
        finished(place, z_sems.at[half])
        for step in (2, 1, 3):
            remote(place, place, x_send, x_sems.at[4 + step], dp=to(step))

    def pass_x(offset):
        place = x.at[rows_of(source(offset))]
        if offset != 4:
            finished(place, x_sems.at[offset])
        remote(place, place, x_send, x_sems.at[CHIPS + offset], dp=sibling)

    first_gram = own_half(0)
    spread_half(0)
    start_x(1, own_half(1) + first_gram)
    spread_half(1)
    pass_half(0)
    start_z(1)
    pass_half(1)

    @pl.when(chip < TAIL_OWNERS)
    def _():
        finished(got_tail.at[pl.ds(0, TAIL_OWNERS - 1)], tailx_sem)

    @pl.when(chip >= TAIL_OWNERS)
    def _():
        finished(got_tail.at[pl.ds(0, TAIL_OWNERS)], tailx_sem)

    remote(x.at[rows_of(tail_block)], x.at[rows_of(tail_block)], tails_send, tails_sem, dp=sibling)

    start_x(0, gram_of(x[rows_of(tail_block)]))
    pass_x(4)
    for offset in (1, 3, 2):
        pass_x(offset)
    start_z(0)

    def send_matrix(block, matrix):
        p[block] = pack(matrix)
        if block is me:
            for offset in order:
                remote(p.at[me], p.at[me], p_send, p_sems.at[offset], dp=to(offset))
        remote(p.at[block], p.at[block], p_send, p_sems.at[0] if block is me else tailp_sem, dp=sibling)

    send_matrix(me, polynomial_of(total_gram(1)))
    for offset in (5, 7, 6):
        pass_x(offset)
    send_matrix(tail_block, polynomial_of(total_gram(0)))

    def apply_at(*blocks):
        results = [applied(x[rows_of(block)], p[block]) for block in blocks]
        for block, result in zip(blocks, results):
            ortho[rows_of(block)] = result

    def pass_p(offset):
        place = p.at[source(offset)]
        finished(place, p_sems.at[offset])
        remote(place, place, p_send, p_sems.at[CHIPS + offset], dp=sibling)

    def other_of(offset):
        return source(offset) + 1 - 2 * core

    finished(x.at[rows_of(sibling)], x_sems.at[0])
    finished(p.at[sibling], p_sems.at[0])
    for offset in (4, 1, 3):
        pass_p(offset)
    apply_at(me, sibling, source(4), source(1), source(3))
    for offset in (5, 7, 2, 6):
        pass_p(offset)
    finished(x.at[rows_of(tail_other)], tails_sem)
    finished(p.at[tail_other], tailp_sem)
    apply_at(tail_block, tail_other, source(5), source(7), source(2), source(6))
    for offset in (4, 1, 3, 5, 7, 2, 6):
        other = other_of(offset)
        finished(x.at[rows_of(other)], x_sems.at[CHIPS + offset])
        finished(p.at[other], p_sems.at[CHIPS + offset])
    apply_at(*(other_of(offset) for offset in (4, 1, 3, 5, 7, 2, 6)))

    keep_params.wait()
    finished(theirs, their_send)
    finished(got_codes.at[pl.ds(1, CHIPS - 1)], code_send)
    finished(got_scales.at[pl.ds(1, CHIPS - 1)], scale_send)

    @pl.when(chip < TAIL_OWNERS)
    def _():
        finished(got_tail.at[pl.ds(0, TAIL_OWNERS - 1)], tail_send)
        finished(got_tail_scales.at[pl.ds(0, TAIL_OWNERS - 1)], tail_scale_send)
        finished(got_tail.at[pl.ds(0, CHIPS - 1)], tailx_send)

    @pl.when(chip >= TAIL_OWNERS)
    def _():
        finished(got_tail.at[pl.ds(0, TAIL_OWNERS)], tail_send)
        finished(got_tail_scales.at[pl.ds(0, TAIL_OWNERS)], tail_scale_send)

    finished(x.at[rows_of(tail_block)], tails_send)
    for which in range(2):
        finished(from_x.at[which], gx_send.at[which])
        finished(from_z.at[which], gz_send.at[which])
    finished(x.at[pl.ds(0, 15 * rows)], x_send)
    finished(p.at[pl.ds(0, 16)], p_send)


def exchange(grads, params, count, rows):
    piece = rows // TAIL_OWNERS
    dma = pltpu.SemaphoreType.DMA
    vmem = pltpu.VMEM
    return pl.pallas_call(
        functools.partial(communicate, count=count, rows=rows),
        out_shape=(
            jax.ShapeDtypeStruct((count * rows, V), jnp.bfloat16),
            jax.ShapeDtypeStruct((count * rows, V), jnp.float32),
        ),
        in_specs=[pl.BlockSpec(memory_space=pltpu.HBM)] * 2,
        out_specs=(pl.BlockSpec(memory_space=vmem), pl.BlockSpec(memory_space=vmem)),
        scratch_shapes=[
            vmem((CHIPS + 1, rows, V), jnp.bfloat16),
            vmem((CHIPS + 1, rows, V), jnp.bfloat16),
            vmem((CHIPS + 1, rows, V), jnp.bfloat16),
            vmem((CHIPS, rows, V), jnp.int16),
            vmem((CHIPS, 8, V), jnp.float32),
            vmem((CHIPS, rows, V), jnp.int16),
            vmem((CHIPS, 8, V), jnp.float32),
            vmem((rows, V), jnp.int16),
            vmem((8, V), jnp.float32),
            vmem((CHIPS, piece, V), jnp.int16),
            vmem((CHIPS, 8, V), jnp.float32),
            vmem((count * rows, V), jnp.bfloat16),
            vmem((count, PACKED, V), jnp.float32),
            vmem((rows, V), jnp.float32),
            vmem((2, 2, PACKED, V), jnp.float32),
            vmem((2, 3, PACKED, V), jnp.float32),
            vmem((2, 3, PACKED, V), jnp.float32),
            dma((CHIPS + 1,)), dma((CHIPS + 1,)), dma((CHIPS + 1,)), dma, dma((2, CHIPS)), dma((CHIPS,)), dma, dma,
            dma, dma, dma, dma, dma, dma, dma, dma,
            dma((2,)), dma((2,)), dma((2,)), dma((2,)),
            dma((2 * CHIPS,)), dma((2,)), dma, dma((2 * CHIPS,)), dma, dma, dma,
        ],
        compiler_params=pltpu.CompilerParams(
            collective_id=0, has_side_effects=True, vmem_limit_bytes=40 * 2**20
        ),
    )(grads, params)


def finish(table, ortho, params, new_params, update, new_held, update_held, sems):
    count = ortho.shape[0]

    def one(j, carry):
        head = table[j]
        scaled = 0.2 * math.sqrt(max(D, V)) * ortho[j].astype(jnp.float32)
        old = params[head]
        new_held[j] = old - learning_rate * (scaled + decay_rate * old)
        update_held[j] = scaled.astype(jnp.bfloat16)
        pltpu.make_async_copy(new_held.at[j], new_params.at[head], sems.at[0]).start()
        pltpu.make_async_copy(update_held.at[j], update.at[head], sems.at[1]).start()
        return carry

    lax.fori_loop(0, count, one, 0)
    pltpu.make_async_copy(new_held, new_params, sems.at[0]).wait()
    pltpu.make_async_copy(update_held, update, sems.at[1]).wait()


def apply(table, ortho, params):
    vmem = pltpu.VMEM
    return pl.pallas_call(
        finish,
        in_specs=[
            pl.BlockSpec(memory_space=pltpu.SMEM),
            pl.BlockSpec(memory_space=vmem),
            pl.BlockSpec(memory_space=vmem),
        ],
        out_specs=(pl.BlockSpec(memory_space=pltpu.HBM), pl.BlockSpec(memory_space=pltpu.HBM)),
        out_shape=(
            jax.ShapeDtypeStruct(params.shape, jnp.float32),
            jax.ShapeDtypeStruct(params.shape, jnp.bfloat16),
        ),
        scratch_shapes=[
            vmem(params.shape, jnp.float32),
            vmem(params.shape, jnp.bfloat16),
            pltpu.SemaphoreType.DMA((2,)),
        ],
        compiler_params=pltpu.CompilerParams(vmem_limit_bytes=32 * 2**20),
    )(table, ortho, params)


def per_device(grads, params, table):
    count, rows, width = params.shape
    flat = (count * rows, width)
    ortho, held = exchange(pltpu.with_memory_space_constraint(grads.reshape(flat), pltpu.HBM), pltpu.with_memory_space_constraint(params.reshape(flat), pltpu.HBM), count, rows)
    return apply(table, ortho.reshape(params.shape), held.reshape(params.shape))


def solution(mesh):
    return jax.shard_map(
        per_device,
        mesh=mesh,
        in_specs=(P("dp", None, "shard", None), P(None, "shard", None), P()),
        out_specs=(P(None, "shard", None), P(None, "shard", None)),
        check_vma=False,
    )
```

```python
import functools
import math

import jax
import jax.numpy as jnp
from jax import lax
from jax.experimental import pallas as pl
from jax.experimental.pallas import tpu as pltpu
from jax.sharding import PartitionSpec as P

D = 7168
V = 128
HALF = V // 2
PACKED = HALF + 8
ITERS = 5
N_DP = 16
CHIPS = 8
TAIL_OWNERS = 7
CODE_MAX = 32767.0

quintic_one = 3.4445
quintic_two = -4.775
quintic_three = 2.0315
epsilon = 1e-07
learning_rate = 0.02
decay_rate = 0.1

MESH = pl.DeviceIdType.MESH


def exact_dot(left, right, precision=lax.Precision.HIGHEST):
    return jnp.dot(left, right, precision=precision, preferred_element_type=jnp.float32)


def places(rows):
    return (
        lax.broadcasted_iota(jnp.int32, (rows, V), 0),
        lax.broadcasted_iota(jnp.int32, (rows, V), 1),
    )


def gram_of(rows):
    return lax.dot_general(
        rows, rows, (((0,), (0,)), ((), ())), preferred_element_type=jnp.float32
    )


def pack(matrix):
    row, col = places(HALF)
    corner = pltpu.roll(matrix[HALF:], HALF, 1)
    body = jnp.where((col < HALF) & (row > col), corner, matrix[:HALF])
    diagonal = jnp.sum(jnp.where(row == col, corner, 0.0), axis=0, keepdims=True)
    return jnp.concatenate([body, jnp.broadcast_to(diagonal, (8, V))], axis=0)


def unpack(packed):
    row, col = places(HALF)
    body, diagonal = packed[:HALF], packed[HALF:HALF + 1]
    turned = jnp.concatenate([body, jnp.zeros_like(body)], axis=0).T
    top = jnp.where((col < HALF) & (row > col), turned[:HALF], body)
    corner = jnp.where(row > col, body, jnp.where(row < col, turned[:HALF], diagonal))
    bottom = jnp.where(col < HALF, turned[HALF:], pltpu.roll(corner, HALF, 1))
    return jnp.concatenate([top, bottom], axis=0)


def polynomial_of(total_gram):
    row, col = places(V)
    eye = (row == col).astype(jnp.float32)
    square = jnp.sum(jnp.sum(total_gram * eye, axis=1, keepdims=True), axis=0, keepdims=True)
    inverse = 1.0 / (jnp.sqrt(square) + epsilon)
    gram = (total_gram * inverse) * inverse
    product = None
    for index in range(ITERS):
        dot = functools.partial(
            exact_dot, precision=lax.Precision.HIGHEST if index < ITERS - 2 else lax.Precision.HIGH
        )
        step = quintic_one * eye + quintic_two * gram + quintic_three * dot(gram, gram)
        if index == ITERS - 1:
            product = dot(product, step)
        elif index == 0:
            product = step
            gram = dot(dot(gram, step), step)
        else:
            both = dot(jnp.concatenate([gram, product], axis=0), step)
            product = both[V:]
            gram = dot(both[:V], step)
    return product * inverse


def coded(total):
    peak = jnp.maximum(jnp.max(jnp.abs(total), axis=0, keepdims=True), 1e-33)
    codes = jnp.round(total * (CODE_MAX / peak)).astype(jnp.int32).astype(jnp.int16)
    return codes, jnp.broadcast_to(peak * (1.0 / CODE_MAX), (8, V))


def decoded(codes, scale):
    return codes.astype(jnp.int32).astype(jnp.float32) * scale


def applied(block, packed):
    matrix = unpack(packed)
    high = matrix.astype(jnp.bfloat16)
    low = (matrix - high.astype(jnp.float32)).astype(jnp.bfloat16)
    return jnp.dot(
        jnp.concatenate([block, block], axis=1),
        jnp.concatenate([high, low], axis=0),
        preferred_element_type=jnp.float32,
    ).astype(jnp.bfloat16)


def communicate(
    grads, params, ortho, held_params,
    mine, given, theirs, codes, scales, got_codes, got_scales,
    tail_codes, tail_scales, got_tail, got_tail_scales,
    x, p, total, sums, from_x, from_z,
    mine_sems, given_sems, their_sems, their_send, code_sems, scale_sems, code_send, scale_send,
    tail_sem, tail_scale_sem, tail_send, tail_scale_send, tailx_sem, tailx_send, tails_sem, tails_send,
    gx_sems, gx_send, gz_sems, gz_send, x_sems, z_sems, x_send, p_sems, p_send, tailp_sem, params_sem,
    *, count, rows,
):
    piece = rows // TAIL_OWNERS
    me = lax.axis_index("dp")
    shard = lax.axis_index("shard")
    core = lax.rem(me, 2)
    chip = me // 2
    sibling = me + 1 - 2 * core
    tail_block = N_DP + core
    tail_other = N_DP + 1 - core

    def chip_at(offset, sign=1):
        z = lax.rem(chip // 4 + offset // 4, 2)
        y = lax.rem(lax.rem(chip, 4) + 4 + sign * (offset % 4), 4)
        return 4 * z + y

    def to(offset):
        return 2 * chip_at(offset) + core

    def source(offset):
        return 2 * chip_at(offset, -1) + core

    def rows_of(block):
        return pl.ds(block * rows, rows)

    def x_peer(step):
        return shard - lax.rem(shard, 4) + lax.rem(lax.rem(shard, 4) + step, 4)

    def z_peer(step):
        return lax.rem(shard // 4 + step, 4) * 4 + lax.rem(shard, 4)

    def remote(src, dst, send_sem, recv_sem, **device):
        pltpu.make_async_remote_copy(
            src_ref=src, dst_ref=dst, send_sem=send_sem, recv_sem=recv_sem,
            device_id=device, device_id_type=MESH,
        ).start()

    def finished(ref, sem):
        pltpu.make_async_copy(ref, ref, sem).wait()

    order = (6, 2, 5, 7, 4, 1, 3)

    barrier = pltpu.get_barrier_semaphore()
    for step in (2, 1, 3):
        pl.semaphore_signal(barrier, inc=1, device_id={"shard": z_peer(step)}, device_id_type=MESH)
    for offset in order:
        pl.semaphore_signal(barrier, inc=1, device_id={"dp": to(offset)}, device_id_type=MESH)
    for step in (2, 1, 3):
        pl.semaphore_signal(barrier, inc=1, device_id={"shard": x_peer(step)}, device_id_type=MESH)
    pl.semaphore_signal(barrier, inc=1, device_id={"dp": sibling}, device_id_type=MESH)

    first_slots = ((CHIPS, tail_block, tail_other),) + tuple(
        (offset, to(offset), to(offset) + 1 - 2 * core) for offset in order + (0,)
    )
    for slot, _, block in first_slots:
        pltpu.make_async_copy(grads.at[rows_of(block)], given.at[slot], given_sems.at[slot]).start()
    for slot, block, _ in first_slots:
        pltpu.make_async_copy(grads.at[rows_of(block)], mine.at[slot], mine_sems.at[slot]).start()
    for slot, _, _ in first_slots:
        finished(given.at[slot], given_sems.at[slot])
    pl.semaphore_wait(barrier, CHIPS + 6)
    for slot, _, _ in first_slots:
        remote(given.at[slot], theirs.at[slot], their_send, their_sems.at[slot], dp=sibling)
    keep_params = pltpu.make_async_copy(params, held_params, params_sem)
    keep_params.start()

    def pair_sum(slot):
        finished(mine.at[slot], mine_sems.at[slot])
        finished(theirs.at[slot], their_sems.at[slot])
        return mine[slot].astype(jnp.float32) + theirs[slot].astype(jnp.float32)

    pair = pair_sum(CHIPS)
    packed, scale = coded(pair)
    tail_codes[...] = packed
    tail_scales[...] = scale
    for offset in order:
        peer = chip_at(offset)

        @pl.when(peer < TAIL_OWNERS)
        def _():
            remote(
                tail_codes.at[pl.ds(peer * piece, piece)], got_tail.at[offset], tail_send, tail_sem,
                dp=2 * peer + core,
            )
            remote(tail_scales, got_tail_scales.at[offset], tail_scale_send, tail_scale_sem, dp=2 * peer + core)

    halves = (pl.ds(0, rows // 2), pl.ds(rows // 2, rows // 2))

    def send_codes(half, offset):
        remote(
            codes.at[offset, halves[half]], got_codes.at[offset, halves[half]], code_send,
            code_sems.at[half, offset], dp=to(offset),
        )

    for offset in order:
        packed, scale = coded(pair_sum(offset))
        codes[offset] = packed
        scales[offset] = scale
        remote(scales.at[offset], got_scales.at[offset], scale_send, scale_sems.at[offset], dp=to(offset))
        send_codes(0, offset)

    for offset in order:
        send_codes(1, offset)

    tail_rows = pl.ds(tail_block * rows + chip * piece, piece)

    @pl.when(chip < TAIL_OWNERS)
    def _():
        here = pl.ds(pl.multiple_of(chip * piece, piece), piece)
        summed = mine[CHIPS, here].astype(jnp.float32) + theirs[CHIPS, here].astype(jnp.float32)
        finished(got_tail.at[pl.ds(1, CHIPS - 1)], tail_sem)
        finished(got_tail_scales.at[pl.ds(1, CHIPS - 1)], tail_scale_sem)
        for offset in range(1, CHIPS):
            summed = summed + decoded(got_tail[offset], got_tail_scales[offset, 0:1])
        x[tail_rows] = summed.astype(jnp.bfloat16)
        for offset in order:
            remote(x.at[tail_rows], x.at[tail_rows], tailx_send, tailx_sem, dp=to(offset))

    total[...] = pair_sum(0)

    chunks = (pl.ds(0, HALF // 2), pl.ds(HALF // 2, PACKED - HALF // 2))

    def start_x(which, gram):
        sums[which, 0] = pack(gram)
        for index, part in enumerate(chunks):
            for step in (2, 1, 3):
                remote(
                    sums.at[which, 0, part], from_x.at[which, step - 1, part], gx_send.at[which],
                    gx_sems.at[which, index], shard=x_peer(step),
                )

    def start_z(which):
        for index, part in enumerate(chunks):
            finished(from_x.at[which, :, part], gx_sems.at[which, index])
            sums[which, 1, part] = (
                sums[which, 0, part] + from_x[which, 0, part] + from_x[which, 1, part] + from_x[which, 2, part]
            )
            for step in (2, 1, 3):
                remote(
                    sums.at[which, 1, part], from_z.at[which, step - 1, part], gz_send.at[which],
                    gz_sems.at[which, index], shard=z_peer(step),
                )

    def total_gram(which):
        for index, part in enumerate(chunks):
            finished(from_z.at[which, :, part], gz_sems.at[which, index])
        return unpack(sums[which, 1] + from_z[which, 0] + from_z[which, 1] + from_z[which, 2])

    def own_half(half):
        here = halves[half]
        for offset in order:
            finished(got_codes.at[offset, here], code_sems.at[half, offset])
            if half == 0:
                finished(got_scales.at[offset], scale_sems.at[offset])
            total[here] = total[here] + decoded(got_codes[offset, here], got_scales[offset, 0:1])
        summed = total[here].astype(jnp.bfloat16)
        x[pl.ds(me * rows + half * (rows // 2), rows // 2)] = summed
        return gram_of(summed)

    def spread_half(half):
        place = x.at[pl.ds(me * rows + half * (rows // 2), rows // 2)]
        remote(place, place, x_send, z_sems.at[half], dp=to(4))
        for offset in (2, 1, 3):
            remote(place, place, x_send, x_sems.at[offset], dp=to(offset))
        remote(place, place, x_send, x_sems.at[0], dp=sibling)

    def pass_half(half):
        place = x.at[pl.ds(source(4) * rows + half * (rows // 2), rows // 2)]
        finished(place, z_sems.at[half])
        for step in (2, 1, 3):
            remote(place, place, x_send, x_sems.at[4 + step], dp=to(step))

    def pass_x(offset):
        place = x.at[rows_of(source(offset))]
        if offset != 4:
            finished(place, x_sems.at[offset])
        remote(place, place, x_send, x_sems.at[CHIPS + offset], dp=sibling)

    first_gram = own_half(0)
    spread_half(0)
    start_x(1, own_half(1) + first_gram)
    spread_half(1)
    pass_half(0)
    start_z(1)
    pass_half(1)

    @pl.when(chip < TAIL_OWNERS)
    def _():
        finished(got_tail.at[pl.ds(0, TAIL_OWNERS - 1)], tailx_sem)

    @pl.when(chip >= TAIL_OWNERS)
    def _():
        finished(got_tail.at[pl.ds(0, TAIL_OWNERS)], tailx_sem)

    remote(x.at[rows_of(tail_block)], x.at[rows_of(tail_block)], tails_send, tails_sem, dp=sibling)

    start_x(0, gram_of(x[rows_of(tail_block)]))
    pass_x(4)
    for offset in (1, 3, 2):
        pass_x(offset)
    start_z(0)

    def send_matrix(block, matrix):
        p[block] = pack(matrix)
        if block is me:
            for offset in order:
                remote(p.at[me], p.at[me], p_send, p_sems.at[offset], dp=to(offset))
        remote(p.at[block], p.at[block], p_send, p_sems.at[0] if block is me else tailp_sem, dp=sibling)

    send_matrix(me, polynomial_of(total_gram(1)))
    for offset in (5, 7, 6):
        pass_x(offset)
    send_matrix(tail_block, polynomial_of(total_gram(0)))

    def apply_at(*blocks):
        results = [applied(x[rows_of(block)], p[block]) for block in blocks]
        for block, result in zip(blocks, results):
            ortho[rows_of(block)] = result

    def pass_p(offset):
        place = p.at[source(offset)]
        finished(place, p_sems.at[offset])
        remote(place, place, p_send, p_sems.at[CHIPS + offset], dp=sibling)

    def other_of(offset):
        return source(offset) + 1 - 2 * core

    finished(x.at[rows_of(sibling)], x_sems.at[0])
    finished(p.at[sibling], p_sems.at[0])
    for offset in (4, 1, 3):
        pass_p(offset)
    apply_at(me, sibling, source(4), source(1), source(3))
    for offset in (5, 7, 2, 6):
        pass_p(offset)
    finished(x.at[rows_of(tail_other)], tails_sem)
    finished(p.at[tail_other], tailp_sem)
    apply_at(tail_block, tail_other, source(5), source(7), source(2), source(6))
    for offset in (4, 1, 3, 5, 7, 2, 6):
        other = other_of(offset)
        finished(x.at[rows_of(other)], x_sems.at[CHIPS + offset])
        finished(p.at[other], p_sems.at[CHIPS + offset])
    apply_at(*(other_of(offset) for offset in (4, 1, 3, 5, 7, 2, 6)))

    keep_params.wait()
    finished(theirs, their_send)
    finished(got_codes.at[pl.ds(1, CHIPS - 1)], code_send)
    finished(got_scales.at[pl.ds(1, CHIPS - 1)], scale_send)

    @pl.when(chip < TAIL_OWNERS)
    def _():
        finished(got_tail.at[pl.ds(0, TAIL_OWNERS - 1)], tail_send)
        finished(got_tail_scales.at[pl.ds(0, TAIL_OWNERS - 1)], tail_scale_send)
        finished(got_tail.at[pl.ds(0, CHIPS - 1)], tailx_send)

    @pl.when(chip >= TAIL_OWNERS)
    def _():
        finished(got_tail.at[pl.ds(0, TAIL_OWNERS)], tail_send)
        finished(got_tail_scales.at[pl.ds(0, TAIL_OWNERS)], tail_scale_send)

    finished(x.at[rows_of(tail_block)], tails_send)
    for which in range(2):
        finished(from_x.at[which], gx_send.at[which])
        finished(from_z.at[which], gz_send.at[which])
    finished(x.at[pl.ds(0, 15 * rows)], x_send)
    finished(p.at[pl.ds(0, 16)], p_send)


def exchange(grads, params, count, rows):
    piece = rows // TAIL_OWNERS
    dma = pltpu.SemaphoreType.DMA
    vmem = pltpu.VMEM
    return pl.pallas_call(
        functools.partial(communicate, count=count, rows=rows),
        out_shape=(
            jax.ShapeDtypeStruct((count * rows, V), jnp.bfloat16),
            jax.ShapeDtypeStruct((count * rows, V), jnp.float32),
        ),
        in_specs=[pl.BlockSpec(memory_space=pltpu.HBM)] * 2,
        out_specs=(pl.BlockSpec(memory_space=vmem), pl.BlockSpec(memory_space=vmem)),
        scratch_shapes=[
            vmem((CHIPS + 1, rows, V), jnp.bfloat16),
            vmem((CHIPS + 1, rows, V), jnp.bfloat16),
            vmem((CHIPS + 1, rows, V), jnp.bfloat16),
            vmem((CHIPS, rows, V), jnp.int16),
            vmem((CHIPS, 8, V), jnp.float32),
            vmem((CHIPS, rows, V), jnp.int16),
            vmem((CHIPS, 8, V), jnp.float32),
            vmem((rows, V), jnp.int16),
            vmem((8, V), jnp.float32),
            vmem((CHIPS, piece, V), jnp.int16),
            vmem((CHIPS, 8, V), jnp.float32),
            vmem((count * rows, V), jnp.bfloat16),
            vmem((count, PACKED, V), jnp.float32),
            vmem((rows, V), jnp.float32),
            vmem((2, 2, PACKED, V), jnp.float32),
            vmem((2, 3, PACKED, V), jnp.float32),
            vmem((2, 3, PACKED, V), jnp.float32),
            dma((CHIPS + 1,)), dma((CHIPS + 1,)), dma((CHIPS + 1,)), dma, dma((2, CHIPS)), dma((CHIPS,)), dma, dma,
            dma, dma, dma, dma, dma, dma, dma, dma,
            dma((2, 2)), dma((2,)), dma((2, 2)), dma((2,)),
            dma((2 * CHIPS,)), dma((2,)), dma, dma((2 * CHIPS,)), dma, dma, dma,
        ],
        compiler_params=pltpu.CompilerParams(
            collective_id=0, has_side_effects=True, vmem_limit_bytes=40 * 2**20
        ),
    )(grads, params)


def finish(table, ortho, params, new_params, update, new_held, update_held, sems):
    count = ortho.shape[0]

    def one(j, carry):
        head = table[j]
        scaled = 0.2 * math.sqrt(max(D, V)) * ortho[j].astype(jnp.float32)
        old = params[head]
        new_held[j] = old - learning_rate * (scaled + decay_rate * old)
        update_held[j] = scaled.astype(jnp.bfloat16)
        pltpu.make_async_copy(new_held.at[j], new_params.at[head], sems.at[0]).start()
        pltpu.make_async_copy(update_held.at[j], update.at[head], sems.at[1]).start()
        return carry

    lax.fori_loop(0, count, one, 0)
    pltpu.make_async_copy(new_held, new_params, sems.at[0]).wait()
    pltpu.make_async_copy(update_held, update, sems.at[1]).wait()


def apply(table, ortho, params):
    vmem = pltpu.VMEM
    return pl.pallas_call(
        finish,
        in_specs=[
            pl.BlockSpec(memory_space=pltpu.SMEM),
            pl.BlockSpec(memory_space=vmem),
            pl.BlockSpec(memory_space=vmem),
        ],
        out_specs=(pl.BlockSpec(memory_space=pltpu.HBM), pl.BlockSpec(memory_space=pltpu.HBM)),
        out_shape=(
            jax.ShapeDtypeStruct(params.shape, jnp.float32),
            jax.ShapeDtypeStruct(params.shape, jnp.bfloat16),
        ),
        scratch_shapes=[
            vmem(params.shape, jnp.float32),
            vmem(params.shape, jnp.bfloat16),
            pltpu.SemaphoreType.DMA((2,)),
        ],
        compiler_params=pltpu.CompilerParams(vmem_limit_bytes=32 * 2**20),
    )(table, ortho, params)


def per_device(grads, params, table):
    count, rows, width = params.shape
    flat = (count * rows, width)
    ortho, held = exchange(pltpu.with_memory_space_constraint(grads.reshape(flat), pltpu.HBM), pltpu.with_memory_space_constraint(params.reshape(flat), pltpu.HBM), count, rows)
    return apply(table, ortho.reshape(params.shape), held.reshape(params.shape))


def solution(mesh):
    return jax.shard_map(
        per_device,
        mesh=mesh,
        in_specs=(P("dp", None, "shard", None), P(None, "shard", None), P()),
        out_specs=(P(None, "shard", None), P(None, "shard", None)),
        check_vma=False,
    )
```

```python
import functools
import math

import jax
import jax.numpy as jnp
from jax import lax
from jax.experimental import pallas as pl
from jax.experimental.pallas import tpu as pltpu
from jax.sharding import PartitionSpec as P

D = 7168
V = 128
HALF = V // 2
PACKED = HALF + 8
ITERS = 5
N_DP = 16
CHIPS = 8
TAIL_OWNERS = 7
CODE_MAX = 32767.0

quintic_one = 3.4445
quintic_two = -4.775
quintic_three = 2.0315
epsilon = 1e-07
learning_rate = 0.02
decay_rate = 0.1

MESH = pl.DeviceIdType.MESH


def exact_dot(left, right):
    return jnp.dot(left, right, precision=lax.Precision.HIGHEST, preferred_element_type=jnp.float32)


def places(rows):
    return (
        lax.broadcasted_iota(jnp.int32, (rows, V), 0),
        lax.broadcasted_iota(jnp.int32, (rows, V), 1),
    )


def gram_of(rows):
    return lax.dot_general(
        rows, rows, (((0,), (0,)), ((), ())), preferred_element_type=jnp.float32
    )


def pack(matrix):
    row, col = places(HALF)
    corner = pltpu.roll(matrix[HALF:], HALF, 1)
    body = jnp.where((col < HALF) & (row > col), corner, matrix[:HALF])
    diagonal = jnp.sum(jnp.where(row == col, corner, 0.0), axis=0, keepdims=True)
    return jnp.concatenate([body, jnp.broadcast_to(diagonal, (8, V))], axis=0)


def unpack(packed):
    row, col = places(HALF)
    body, diagonal = packed[:HALF], packed[HALF:HALF + 1]
    turned = jnp.concatenate([body, jnp.zeros_like(body)], axis=0).T
    top = jnp.where((col < HALF) & (row > col), turned[:HALF], body)
    corner = jnp.where(row > col, body, jnp.where(row < col, turned[:HALF], diagonal))
    bottom = jnp.where(col < HALF, turned[HALF:], pltpu.roll(corner, HALF, 1))
    return jnp.concatenate([top, bottom], axis=0)


def polynomial_of(total_gram):
    row, col = places(V)
    eye = (row == col).astype(jnp.float32)
    square = jnp.sum(jnp.sum(total_gram * eye, axis=1, keepdims=True), axis=0, keepdims=True)
    inverse = 1.0 / (jnp.sqrt(square) + epsilon)
    gram = (total_gram * inverse) * inverse
    product = None
    for index in range(ITERS):
        step = quintic_one * eye + quintic_two * gram + quintic_three * exact_dot(gram, gram)
        if index == ITERS - 1:
            product = exact_dot(product, step)
        elif index == 0:
            product = step
            gram = exact_dot(exact_dot(gram, step), step)
        else:
            both = exact_dot(jnp.concatenate([gram, product], axis=0), step)
            product = both[V:]
            gram = exact_dot(both[:V], step)
    return product * inverse


def coded(total):
    peak = jnp.maximum(jnp.max(jnp.abs(total), axis=0, keepdims=True), 1e-33)
    codes = jnp.round(total * (CODE_MAX / peak)).astype(jnp.int32).astype(jnp.int16)
    return codes, jnp.broadcast_to(peak * (1.0 / CODE_MAX), (8, V))


def decoded(codes, scale):
    return codes.astype(jnp.int32).astype(jnp.float32) * scale


def applied(block, packed):
    matrix = unpack(packed)
    high = matrix.astype(jnp.bfloat16)
    low = (matrix - high.astype(jnp.float32)).astype(jnp.bfloat16)
    return jnp.dot(
        jnp.concatenate([block, block], axis=1),
        jnp.concatenate([high, low], axis=0),
        preferred_element_type=jnp.float32,
    ).astype(jnp.bfloat16)


def communicate(
    grads, params, ortho, held_params,
    mine, given, theirs, codes, scales, got_codes, got_scales,
    tail_codes, tail_scales, got_tail, got_tail_scales,
    x, p, total, sums, from_x, from_z,
    mine_sems, given_sems, their_sems, their_send, code_sems, scale_sems, code_send, scale_send,
    tail_sem, tail_scale_sem, tail_send, tail_scale_send, tailx_sem, tailx_send, tails_sem, tails_send,
    gx_sems, gx_send, gz_sems, gz_send, x_sems, z_sems, x_send, p_sems, p_send, tailp_sem, params_sem,
    *, count, rows,
):
    piece = rows // TAIL_OWNERS
    me = lax.axis_index("dp")
    shard = lax.axis_index("shard")
    core = lax.rem(me, 2)
    chip = me // 2
    sibling = me + 1 - 2 * core
    tail_block = N_DP + core
    tail_other = N_DP + 1 - core

    def chip_at(offset, sign=1):
        z = lax.rem(chip // 4 + offset // 4, 2)
        y = lax.rem(lax.rem(chip, 4) + 4 + sign * (offset % 4), 4)
        return 4 * z + y

    def to(offset):
        return 2 * chip_at(offset) + core

    def source(offset):
        return 2 * chip_at(offset, -1) + core

    def rows_of(block):
        return pl.ds(block * rows, rows)

    def x_peer(step):
        return shard - lax.rem(shard, 4) + lax.rem(lax.rem(shard, 4) + step, 4)

    def z_peer(step):
        return lax.rem(shard // 4 + step, 4) * 4 + lax.rem(shard, 4)

    def remote(src, dst, send_sem, recv_sem, **device):
        pltpu.make_async_remote_copy(
            src_ref=src, dst_ref=dst, send_sem=send_sem, recv_sem=recv_sem,
            device_id=device, device_id_type=MESH,
        ).start()

    def finished(ref, sem):
        pltpu.make_async_copy(ref, ref, sem).wait()

    order = (6, 2, 5, 7, 4, 1, 3)

    barrier = pltpu.get_barrier_semaphore()
    for step in (2, 1, 3):
        pl.semaphore_signal(barrier, inc=1, device_id={"shard": z_peer(step)}, device_id_type=MESH)
    for offset in order:
        pl.semaphore_signal(barrier, inc=1, device_id={"dp": to(offset)}, device_id_type=MESH)
    for step in (2, 1, 3):
        pl.semaphore_signal(barrier, inc=1, device_id={"shard": x_peer(step)}, device_id_type=MESH)
    pl.semaphore_signal(barrier, inc=1, device_id={"dp": sibling}, device_id_type=MESH)

    first_slots = ((CHIPS, tail_block, tail_other),) + tuple(
        (offset, to(offset), to(offset) + 1 - 2 * core) for offset in order + (0,)
    )
    for slot, _, block in first_slots:
        pltpu.make_async_copy(grads.at[rows_of(block)], given.at[slot], given_sems.at[slot]).start()
    for slot, block, _ in first_slots:
        pltpu.make_async_copy(grads.at[rows_of(block)], mine.at[slot], mine_sems.at[slot]).start()
    for slot, _, _ in first_slots:
        finished(given.at[slot], given_sems.at[slot])
    pl.semaphore_wait(barrier, CHIPS + 6)
    for slot, _, _ in first_slots:
        remote(given.at[slot], theirs.at[slot], their_send, their_sems.at[slot], dp=sibling)
    keep_params = pltpu.make_async_copy(params, held_params, params_sem)
    keep_params.start()

    def pair_sum(slot):
        finished(mine.at[slot], mine_sems.at[slot])
        finished(theirs.at[slot], their_sems.at[slot])
        return mine[slot].astype(jnp.float32) + theirs[slot].astype(jnp.float32)

    pair = pair_sum(CHIPS)
    packed, scale = coded(pair)
    tail_codes[...] = packed
    tail_scales[...] = scale
    for offset in order:
        peer = chip_at(offset)

        @pl.when(peer < TAIL_OWNERS)
        def _():
            remote(
                tail_codes.at[pl.ds(peer * piece, piece)], got_tail.at[offset], tail_send, tail_sem,
                dp=2 * peer + core,
            )
            remote(tail_scales, got_tail_scales.at[offset], tail_scale_send, tail_scale_sem, dp=2 * peer + core)

    halves = (pl.ds(0, rows // 2), pl.ds(rows // 2, rows // 2))

    def send_codes(half, offset):
        remote(
            codes.at[offset, halves[half]], got_codes.at[offset, halves[half]], code_send,
            code_sems.at[half, offset], dp=to(offset),
        )

    for offset in order:
        packed, scale = coded(pair_sum(offset))
        codes[offset] = packed
        scales[offset] = scale
        remote(scales.at[offset], got_scales.at[offset], scale_send, scale_sems.at[offset], dp=to(offset))
        send_codes(0, offset)

    for offset in order:
        send_codes(1, offset)

    tail_rows = pl.ds(tail_block * rows + chip * piece, piece)

    @pl.when(chip < TAIL_OWNERS)
    def _():
        here = pl.ds(pl.multiple_of(chip * piece, piece), piece)
        summed = mine[CHIPS, here].astype(jnp.float32) + theirs[CHIPS, here].astype(jnp.float32)
        finished(got_tail.at[pl.ds(1, CHIPS - 1)], tail_sem)
        finished(got_tail_scales.at[pl.ds(1, CHIPS - 1)], tail_scale_sem)
        for offset in range(1, CHIPS):
            summed = summed + decoded(got_tail[offset], got_tail_scales[offset, 0:1])
        x[tail_rows] = summed.astype(jnp.bfloat16)
        for offset in order:
            remote(x.at[tail_rows], x.at[tail_rows], tailx_send, tailx_sem, dp=to(offset))

    total[...] = pair_sum(0)

    def start_x(which, gram):
        sums[which, 0] = pack(gram)
        for step in (2, 1, 3):
            remote(
                sums.at[which, 0], from_x.at[which, step - 1], gx_send.at[which], gx_sems.at[which],
                shard=x_peer(step),
            )

    def start_z(which):
        finished(from_x.at[which], gx_sems.at[which])
        sums[which, 1] = sums[which, 0] + from_x[which, 0] + from_x[which, 1] + from_x[which, 2]
        for step in (2, 1, 3):
            remote(
                sums.at[which, 1], from_z.at[which, step - 1], gz_send.at[which], gz_sems.at[which],
                shard=z_peer(step),
            )

    def total_gram(which):
        finished(from_z.at[which], gz_sems.at[which])
        return unpack(sums[which, 1] + from_z[which, 0] + from_z[which, 1] + from_z[which, 2])

    def own_half(half):
        here = halves[half]
        for offset in order:
            finished(got_codes.at[offset, here], code_sems.at[half, offset])
            if half == 0:
                finished(got_scales.at[offset], scale_sems.at[offset])
            total[here] = total[here] + decoded(got_codes[offset, here], got_scales[offset, 0:1])
        summed = total[here].astype(jnp.bfloat16)
        x[pl.ds(me * rows + half * (rows // 2), rows // 2)] = summed
        return gram_of(summed)

    def spread_half(half):
        place = x.at[pl.ds(me * rows + half * (rows // 2), rows // 2)]
        remote(place, place, x_send, z_sems.at[half], dp=to(4))
        for offset in (2, 1, 3):
            remote(place, place, x_send, x_sems.at[offset], dp=to(offset))
        remote(place, place, x_send, x_sems.at[0], dp=sibling)

    def pass_half(half):
        place = x.at[pl.ds(source(4) * rows + half * (rows // 2), rows // 2)]
        finished(place, z_sems.at[half])
        for step in (2, 1, 3):
            remote(place, place, x_send, x_sems.at[4 + step], dp=to(step))

    def pass_x(offset):
        place = x.at[rows_of(source(offset))]
        if offset != 4:
            finished(place, x_sems.at[offset])
        remote(place, place, x_send, x_sems.at[CHIPS + offset], dp=sibling)

    first_gram = own_half(0)
    spread_half(0)
    start_x(1, own_half(1) + first_gram)
    spread_half(1)
    pass_half(0)
    start_z(1)
    pass_half(1)

    @pl.when(chip < TAIL_OWNERS)
    def _():
        finished(got_tail.at[pl.ds(0, TAIL_OWNERS - 1)], tailx_sem)

    @pl.when(chip >= TAIL_OWNERS)
    def _():
        finished(got_tail.at[pl.ds(0, TAIL_OWNERS)], tailx_sem)

    remote(x.at[rows_of(tail_block)], x.at[rows_of(tail_block)], tails_send, tails_sem, dp=sibling)

    start_x(0, gram_of(x[rows_of(tail_block)]))
    pass_x(4)
    for offset in (1, 3, 2):
        pass_x(offset)
    start_z(0)

    def send_matrix(block, matrix):
        p[block] = pack(matrix)
        if block is me:
            for offset in order:
                remote(p.at[me], p.at[me], p_send, p_sems.at[offset], dp=to(offset))
        remote(p.at[block], p.at[block], p_send, p_sems.at[0] if block is me else tailp_sem, dp=sibling)

    send_matrix(me, polynomial_of(total_gram(1)))
    for offset in (5, 7, 6):
        pass_x(offset)
    send_matrix(tail_block, polynomial_of(total_gram(0)))

    def apply_at(*blocks):
        results = [applied(x[rows_of(block)], p[block]) for block in blocks]
        for block, result in zip(blocks, results):
            ortho[rows_of(block)] = result

    def pass_p(offset):
        place = p.at[source(offset)]
        finished(place, p_sems.at[offset])
        remote(place, place, p_send, p_sems.at[CHIPS + offset], dp=sibling)

    def other_of(offset):
        return source(offset) + 1 - 2 * core

    finished(x.at[rows_of(sibling)], x_sems.at[0])
    finished(p.at[sibling], p_sems.at[0])
    for offset in (4, 1, 3):
        pass_p(offset)
    apply_at(me, sibling, source(4), source(1), source(3))
    for offset in (5, 7, 2, 6):
        pass_p(offset)
    finished(x.at[rows_of(tail_other)], tails_sem)
    finished(p.at[tail_other], tailp_sem)

    def other_here(offset):
        other = other_of(offset)
        finished(x.at[rows_of(other)], x_sems.at[CHIPS + offset])
        finished(p.at[other], p_sems.at[CHIPS + offset])
        return other

    early = [other_here(offset) for offset in (4, 1, 3)]
    apply_at(tail_block, tail_other, source(5), source(7), source(2), source(6), *early)
    apply_at(*(other_here(offset) for offset in (5, 7, 2, 6)))

    keep_params.wait()
    finished(theirs, their_send)
    finished(got_codes.at[pl.ds(1, CHIPS - 1)], code_send)
    finished(got_scales.at[pl.ds(1, CHIPS - 1)], scale_send)

    @pl.when(chip < TAIL_OWNERS)
    def _():
        finished(got_tail.at[pl.ds(0, TAIL_OWNERS - 1)], tail_send)
        finished(got_tail_scales.at[pl.ds(0, TAIL_OWNERS - 1)], tail_scale_send)
        finished(got_tail.at[pl.ds(0, CHIPS - 1)], tailx_send)

    @pl.when(chip >= TAIL_OWNERS)
    def _():
        finished(got_tail.at[pl.ds(0, TAIL_OWNERS)], tail_send)
        finished(got_tail_scales.at[pl.ds(0, TAIL_OWNERS)], tail_scale_send)

    finished(x.at[rows_of(tail_block)], tails_send)
    for which in range(2):
        finished(from_x.at[which], gx_send.at[which])
        finished(from_z.at[which], gz_send.at[which])
    finished(x.at[pl.ds(0, 15 * rows)], x_send)
    finished(p.at[pl.ds(0, 16)], p_send)


def exchange(grads, params, count, rows):
    piece = rows // TAIL_OWNERS
    dma = pltpu.SemaphoreType.DMA
    vmem = pltpu.VMEM
    return pl.pallas_call(
        functools.partial(communicate, count=count, rows=rows),
        out_shape=(
            jax.ShapeDtypeStruct((count * rows, V), jnp.bfloat16),
            jax.ShapeDtypeStruct((count * rows, V), jnp.float32),
        ),
        in_specs=[pl.BlockSpec(memory_space=pltpu.HBM)] * 2,
        out_specs=(pl.BlockSpec(memory_space=vmem), pl.BlockSpec(memory_space=vmem)),
        scratch_shapes=[
            vmem((CHIPS + 1, rows, V), jnp.bfloat16),
            vmem((CHIPS + 1, rows, V), jnp.bfloat16),
            vmem((CHIPS + 1, rows, V), jnp.bfloat16),
            vmem((CHIPS, rows, V), jnp.int16),
            vmem((CHIPS, 8, V), jnp.float32),
            vmem((CHIPS, rows, V), jnp.int16),
            vmem((CHIPS, 8, V), jnp.float32),
            vmem((rows, V), jnp.int16),
            vmem((8, V), jnp.float32),
            vmem((CHIPS, piece, V), jnp.int16),
            vmem((CHIPS, 8, V), jnp.float32),
            vmem((count * rows, V), jnp.bfloat16),
            vmem((count, PACKED, V), jnp.float32),
            vmem((rows, V), jnp.float32),
            vmem((2, 2, PACKED, V), jnp.float32),
            vmem((2, 3, PACKED, V), jnp.float32),
            vmem((2, 3, PACKED, V), jnp.float32),
            dma((CHIPS + 1,)), dma((CHIPS + 1,)), dma((CHIPS + 1,)), dma, dma((2, CHIPS)), dma((CHIPS,)), dma, dma,
            dma, dma, dma, dma, dma, dma, dma, dma,
            dma((2,)), dma((2,)), dma((2,)), dma((2,)),
            dma((2 * CHIPS,)), dma((2,)), dma, dma((2 * CHIPS,)), dma, dma, dma,
        ],
        compiler_params=pltpu.CompilerParams(
            collective_id=0, has_side_effects=True, vmem_limit_bytes=40 * 2**20
        ),
    )(grads, params)


def finish(table, ortho, params, new_params, update, new_held, update_held, sems):
    count = ortho.shape[0]

    def one(j, carry):
        head = table[j]
        scaled = 0.2 * math.sqrt(max(D, V)) * ortho[j].astype(jnp.float32)
        old = params[head]
        new_held[j] = old - learning_rate * (scaled + decay_rate * old)
        update_held[j] = scaled.astype(jnp.bfloat16)
        pltpu.make_async_copy(new_held.at[j], new_params.at[head], sems.at[0]).start()
        pltpu.make_async_copy(update_held.at[j], update.at[head], sems.at[1]).start()
        return carry

    lax.fori_loop(0, count, one, 0, unroll=3)
    pltpu.make_async_copy(new_held, new_params, sems.at[0]).wait()
    pltpu.make_async_copy(update_held, update, sems.at[1]).wait()


def apply(table, ortho, params):
    vmem = pltpu.VMEM
    return pl.pallas_call(
        finish,
        in_specs=[
            pl.BlockSpec(memory_space=pltpu.SMEM),
            pl.BlockSpec(memory_space=vmem),
            pl.BlockSpec(memory_space=vmem),
        ],
        out_specs=(pl.BlockSpec(memory_space=pltpu.HBM), pl.BlockSpec(memory_space=pltpu.HBM)),
        out_shape=(
            jax.ShapeDtypeStruct(params.shape, jnp.float32),
            jax.ShapeDtypeStruct(params.shape, jnp.bfloat16),
        ),
        scratch_shapes=[
            vmem(params.shape, jnp.float32),
            vmem(params.shape, jnp.bfloat16),
            pltpu.SemaphoreType.DMA((2,)),
        ],
        compiler_params=pltpu.CompilerParams(vmem_limit_bytes=32 * 2**20),
    )(table, ortho, params)


def per_device(grads, params, table):
    count, rows, width = params.shape
    flat = (count * rows, width)
    ortho, held = exchange(pltpu.with_memory_space_constraint(grads.reshape(flat), pltpu.HBM), pltpu.with_memory_space_constraint(params.reshape(flat), pltpu.HBM), count, rows)
    return apply(table, ortho.reshape(params.shape), held.reshape(params.shape))


def solution(mesh):
    return jax.shard_map(
        per_device,
        mesh=mesh,
        in_specs=(P("dp", None, "shard", None), P(None, "shard", None), P()),
        out_specs=(P(None, "shard", None), P(None, "shard", None)),
        check_vma=False,
    )
```
